32 devices in a mesh: grp: 4 (over y, core), dev: 8 (over z, x).
Axes of the slice: x: 2, y: 2, z: 4, core: 2. Of those that a mesh axis runs over, the one named last changes fastest.
Arguments:
- video_in: bfloat16 [4, 32, 256, 1024], P(None, ('grp', 'dev')), may hold values from -24 to 24
- space_gain: float32 [1024], replicated, may hold values from 0.25 to 1.75
- space_project: bfloat16 [1024, 1536], replicated, may hold values from -6 to 6
- space_output: bfloat16 [512, 1024], replicated, may hold values from -0.25 to 0.25
- time_gain: float32 [1024], replicated, may hold values from 0.25 to 1.75
- time_project: bfloat16 [1024, 1536], replicated, may hold values from -6 to 6
- time_output: bfloat16 [512, 1024], replicated, may hold values from -0.25 to 0.25
Outputs:
- video_out: bfloat16 [4, 32, 256, 1024], P(None, ('grp', 'dev'))
The draws below stay inside these ranges and needn't reach their ends.
All inputs are finite; a program needn't handle non-finite values.
Results may differ from the reference program's by a relative error of at most 0.007.
Values may be sent and summed in bfloat16 or wider, within the bound.
No kernel may reach another device: no remote copies, remote signals or barrier semaphores. Data moves between devices by JAX's collectives and lax.ppermute only.
A program may use at most 128 MiB of HBM per device.

```python
from functools import partial
import jax
import jax.numpy as jnp
from jax import lax

D = 1024
HEADS = 8
HEAD_DIM = 64
PATCHES = 256
CLIPS = 4
FRAMES = 32


def clipped_normal(key, shape):
    return jnp.clip(jax.random.normal(key, shape, jnp.float32), -4.0, 4.0)


def drawn_draw(key):
    attn_width = HEADS * HEAD_DIM
    subkeys = jax.random.split(key, 1)
    entries_draw = clipped_normal(subkeys[0], (D, 3 * attn_width)) * D ** (-0.5)
    return jnp.clip(entries_draw, -6.0, 6.0)


def draw_space_project(key, part):
    return drawn_draw(jax.random.fold_in(key, 11)).astype(jnp.bfloat16)


def draw_time_project(key, part):
    return drawn_draw(jax.random.fold_in(key, 23)).astype(jnp.bfloat16)


def draw_video_in(key, part):
    subkeys = jax.random.split(jax.random.fold_in(key, 37), 1)
    full_shape = (CLIPS, FRAMES, PATCHES, D)
    entries_draw = clipped_normal(subkeys[0], full_shape)
    return jnp.clip(entries_draw, -24.0, 24.0).astype(jnp.bfloat16)


def noise(own_key, dims, deviation, most, dtype=jnp.bfloat16):
    drawn = deviation * jax.random.normal(own_key, dims, jnp.float32)
    return jnp.clip(drawn, min=-most, max=most).astype(dtype)


def setup_inputs(seed: int = 0) -> dict:
    key_of = jax.random.split(jax.random.key(seed), 8)
    video_in = draw_video_in(jax.random.fold_in(key_of[7], 71), 0)
    space_gain = jnp.clip(1.0 + 0.15 * jax.random.normal(key_of[1], (D,), jnp.float32), 0.25, 1.75)
    space_project = draw_space_project(jax.random.fold_in(key_of[7], 71), 0)
    space_output = noise(key_of[3], (HEADS * HEAD_DIM, D), (HEADS * HEAD_DIM) ** -0.5, 0.25)
    time_gain = jnp.clip(1.0 + 0.15 * jax.random.normal(key_of[4], (D,), jnp.float32), 0.25, 1.75)
    time_project = draw_time_project(jax.random.fold_in(key_of[7], 71), 0)
    time_output = noise(key_of[6], (HEADS * HEAD_DIM, D), (HEADS * HEAD_DIM) ** -0.5, 0.25)
    return dict(video_in=video_in, space_gain=space_gain, space_project=space_project, space_output=space_output, time_gain=time_gain, time_project=time_project, time_output=time_output)


norm_epsilon = 1e-06
masked_score = -1e+30

def layer_norm(activations, gain_vec):
    floats = activations.astype(jnp.float32)
    centre = lax.optimization_barrier(jnp.mean(floats, axis=-1, keepdims=True))
    spread = lax.optimization_barrier(jnp.mean(jnp.square(floats - centre), axis=-1, keepdims=True))
    return ((floats - centre) * lax.rsqrt(spread + norm_epsilon) * gain_vec).astype(jnp.bfloat16)

def soft_weights(scores, allowed):
    scores = jnp.where(allowed, scores, masked_score)
    top_score = lax.optimization_barrier(jnp.max(scores, axis=-1, keepdims=True))
    exponent = jnp.where(allowed, jnp.exp(scores - top_score), 0.0)
    row_total = lax.optimization_barrier(jnp.sum(exponent, axis=-1, keepdims=True))
    return (exponent / row_total).astype(jnp.bfloat16)

def spatial_frame(frame_in, space_gain, space_project, space_output):
    attn_width = HEADS * HEAD_DIM
    normed = layer_norm(frame_in, space_gain)
    projected = jnp.dot(normed.reshape(-1, D), space_project, preferred_element_type=jnp.float32)
    projected = projected.astype(jnp.bfloat16).reshape(CLIPS, PATCHES, 3, HEADS, HEAD_DIM)
    queries = projected[:, :, 0].astype(jnp.float32)
    keys_all = projected[:, :, 1].astype(jnp.float32)
    values_all = projected[:, :, 2].astype(jnp.float32)
    scores = jnp.einsum('cqhe,ckhe->chqk', queries, keys_all) * HEAD_DIM ** (-0.5)
    allowed = jnp.ones((PATCHES, PATCHES), jnp.bool_)
    weights = soft_weights(scores, allowed)
    context = jnp.einsum('chqk,ckhe->cqhe', weights.astype(jnp.float32), values_all).astype(jnp.bfloat16)
    update = jnp.dot(context.reshape(-1, attn_width), space_output, preferred_element_type=jnp.float32)
    return (frame_in.astype(jnp.float32) + update.reshape(CLIPS, PATCHES, D)).astype(jnp.bfloat16)

def temporal_patch(patch_in, time_gain, time_project, time_output):
    attn_width = HEADS * HEAD_DIM
    normed = layer_norm(patch_in, time_gain)
    projected = jnp.dot(normed.reshape(-1, D), time_project, preferred_element_type=jnp.float32)
    projected = projected.astype(jnp.bfloat16).reshape(CLIPS, FRAMES, 3, HEADS, HEAD_DIM)
    queries = projected[:, :, 0].astype(jnp.float32)
    keys_all = projected[:, :, 1].astype(jnp.float32)
    values_all = projected[:, :, 2].astype(jnp.float32)
    scores = jnp.einsum('cqhe,ckhe->chqk', queries, keys_all) * HEAD_DIM ** (-0.5)
    allowed = jnp.arange(FRAMES)[None, :] <= jnp.arange(FRAMES)[:, None]
    weights = soft_weights(scores, allowed)
    context = jnp.einsum('chqk,ckhe->cqhe', weights.astype(jnp.float32), values_all).astype(jnp.bfloat16)
    update = jnp.dot(context.reshape(-1, attn_width), time_output, preferred_element_type=jnp.float32)
    update_rows = update.astype(jnp.bfloat16).reshape(CLIPS, FRAMES, D)
    return (patch_in.astype(jnp.float32) + update_rows.astype(jnp.float32)).astype(jnp.bfloat16)

def reference(video_in, space_gain, space_project, space_output, time_gain, time_project, time_output):
    frames_first = jnp.moveaxis(video_in, 1, 0)
    spatial_fn = partial(spatial_frame, space_gain=space_gain, space_project=space_project, space_output=space_output)
    mixed_rows = lax.map(spatial_fn, frames_first)
    by_patch = jnp.transpose(mixed_rows, (2, 1, 0, 3))
    temporal_fn = partial(temporal_patch, time_gain=time_gain, time_project=time_project, time_output=time_output)
    result = lax.map(temporal_fn, by_patch)
    return jnp.transpose(result, (1, 2, 0, 3))
```

```python
from functools import partial

import jax
import jax.numpy as jnp
from jax import lax
from jax.experimental import pallas as pl
from jax.experimental.pallas import tpu as pltpu
from jax.sharding import PartitionSpec as P

HEADS = 8
HEAD_DIM = 64
WIDTH = HEADS * HEAD_DIM
LANES = 128
EPSILON = 1e-06
MASKED = -1e30
AXES = ("grp", "dev")
CHUNKS = (2, 2)
VMEM_LIMIT = 40 * 1024 * 1024


def normed(floats, gain):
    centred = floats - jnp.mean(floats, axis=-1, keepdims=True)
    spread = jnp.mean(jnp.square(centred), axis=-1, keepdims=True)
    return centred * lax.rsqrt(spread + EPSILON) * gain


def attend(heads, bias):
    rows = heads.shape[0]
    low = lax.broadcasted_iota(jnp.int32, (rows, LANES), 1) < HEAD_DIM
    ones = jnp.ones((rows, LANES), jnp.bfloat16)
    contexts = []
    for pair in range(WIDTH // LANES):
        at = pair * LANES
        queries = heads[:, at : at + LANES] * jnp.bfloat16(HEAD_DIM**-0.5)
        keys = heads[:, WIDTH + at : WIDTH + at + LANES]
        values = heads[:, 2 * WIDTH + at : 2 * WIDTH + at + LANES]
        nothing = jnp.zeros_like(queries)
        stacked = jnp.concatenate([jnp.where(low, queries, nothing), jnp.where(low, nothing, queries)], axis=0)
        scores = lax.dot_general(stacked, keys, (((1,), (1,)), ((), ())), preferred_element_type=jnp.float32)
        if bias is not None:
            scores = scores + jnp.concatenate([bias, bias], axis=0)
        weights = jnp.exp(scores - jnp.max(scores, axis=-1, keepdims=True)).astype(jnp.bfloat16)
        sums = jnp.dot(weights, jnp.concatenate([values, ones], axis=1), preferred_element_type=jnp.float32)
        context = sums[:, :LANES] / sums[:, LANES:]
        contexts.append(jnp.where(low, context[:rows], context[rows:]))
    return jnp.concatenate(contexts, axis=1).astype(jnp.bfloat16)


def space_kernel(video_ref, gain_ref, project_ref, output_ref, time_gain_ref, mixed_ref, sent_ref):
    floats = video_ref[0].astype(jnp.float32)
    heads = jnp.dot(
        normed(floats, gain_ref[...]).astype(jnp.bfloat16), project_ref[...], preferred_element_type=jnp.float32
    ).astype(jnp.bfloat16)
    context = attend(heads, None)
    mixed = (floats + jnp.dot(context, output_ref[...], preferred_element_type=jnp.float32)).astype(jnp.bfloat16)
    mixed_ref[0] = mixed
    sent = normed(mixed.astype(jnp.float32), time_gain_ref[...])
    sent_ref[...] = sent.reshape(sent_ref.shape).astype(jnp.bfloat16)


def time_kernel(patch_here, rows_ref, project_ref, context_ref, bias_ref):
    rows, width = bias_ref.shape[0], rows_ref.shape[-1]

    @pl.when(pl.program_id(0) == 0)
    def _():
        query = lax.broadcasted_iota(jnp.int32, (rows, rows), 0)
        key = lax.broadcasted_iota(jnp.int32, (rows, rows), 1)
        seen = (key <= query) & (lax.rem(query, patch_here) == lax.rem(key, patch_here))
        bias_ref[...] = jnp.where(seen, 0.0, MASKED)

    arrived = rows_ref[...].astype(jnp.float32).reshape(rows, width).astype(jnp.bfloat16)
    heads = jnp.dot(arrived, project_ref[...], preferred_element_type=jnp.float32).astype(jnp.bfloat16)
    context = attend(heads, bias_ref[...])
    context_ref[...] = context.astype(jnp.float32).reshape(context_ref.shape).astype(jnp.bfloat16)


def final_kernel(mixed_ref, context_ref, output_ref, out_ref):
    rows = mixed_ref.shape[1]
    context = context_ref[...].astype(jnp.float32).reshape(rows, WIDTH).astype(jnp.bfloat16)
    update = jnp.dot(context, output_ref[...], preferred_element_type=jnp.float32)
    out_ref[0] = (mixed_ref[0].astype(jnp.float32) + update).astype(jnp.bfloat16)


def whole(shape):
    return pl.BlockSpec(shape, lambda c: (0,) * len(shape))


def exchange_spec(count, patch_here, width):
    if patch_here % 8:
        return pl.BlockSpec((1, count * patch_here, width), lambda c: (c, 0, 0))
    return pl.BlockSpec((count, 1, patch_here, width), lambda c: (0, c, 0, 0))


def exchange_shape(count, clips, patch_here, width):
    if patch_here % 8:
        return jax.ShapeDtypeStruct((clips, count * patch_here, width), jnp.bfloat16)
    return jax.ShapeDtypeStruct((count, clips, patch_here, width), jnp.bfloat16)


def exchange(sent, count, patch_here):
    plain = sent.ndim == 3
    if plain:
        clips, _, width = sent.shape
        sent = sent.reshape(clips, count, patch_here, width).transpose(1, 0, 2, 3)
    arrived = lax.all_to_all(sent, AXES, split_axis=0, concat_axis=0, tiled=True)
    if plain:
        arrived = arrived.transpose(1, 0, 2, 3).reshape(clips, count * patch_here, width)
    return arrived


def cost(macs, bytes_accessed, exps):
    return pl.CostEstimate(flops=2 * macs, bytes_accessed=bytes_accessed, transcendentals=exps)


def space_call(video, first, clips, space_gain, space_project, space_output, time_gain, count):
    rows, width = video.shape[1:]
    patch_here = rows // count
    return pl.pallas_call(
        space_kernel,
        grid=(clips,),
        in_specs=[
            pl.BlockSpec((1, rows, width), lambda c: (first + c, 0, 0)),
            whole((1, width)),
            whole((width, 3 * WIDTH)),
            whole((WIDTH, width)),
            whole((1, width)),
        ],
        out_specs=[
            pl.BlockSpec((1, rows, width), lambda c: (c, 0, 0)),
            exchange_spec(count, patch_here, width),
        ],
        out_shape=[
            jax.ShapeDtypeStruct((clips, rows, width), jnp.bfloat16),
            exchange_shape(count, clips, patch_here, width),
        ],
        cost_estimate=cost(
            clips * rows * (width * 4 * WIDTH + 8 * rows * WIDTH), 2 * (4 * width * WIDTH + 3 * clips * rows * width),
            clips * HEADS * rows * rows,
        ),
        compiler_params=pltpu.CompilerParams(vmem_limit_bytes=VMEM_LIMIT),
        name="space",
    )(video, space_gain, space_project, space_output, time_gain)


def time_call(arrived, clips, rows, time_project, count):
    width = arrived.shape[-1]
    patch_here = rows // count
    return pl.pallas_call(
        partial(time_kernel, patch_here),
        grid=(clips,),
        in_specs=[exchange_spec(count, patch_here, width), whole((width, 3 * WIDTH))],
        out_specs=exchange_spec(count, patch_here, WIDTH),
        out_shape=exchange_shape(count, clips, patch_here, WIDTH),
        scratch_shapes=[pltpu.VMEM((rows, rows), jnp.float32)],
        cost_estimate=cost(
            clips * rows * (width * 3 * WIDTH + 8 * rows * WIDTH), 2 * (3 * width * WIDTH + 2 * clips * rows * width),
            clips * HEADS * rows * rows,
        ),
        compiler_params=pltpu.CompilerParams(vmem_limit_bytes=VMEM_LIMIT),
        name="time",
    )(arrived, time_project)


def final_call(mixed, context, time_output, count):
    clips, rows, width = mixed.shape
    return pl.pallas_call(
        final_kernel,
        grid=(clips,),
        in_specs=[
            pl.BlockSpec((1, rows, width), lambda c: (c, 0, 0)),
            exchange_spec(count, rows // count, WIDTH),
            whole((WIDTH, width)),
        ],
        out_specs=pl.BlockSpec((1, rows, width), lambda c: (c, 0, 0)),
        out_shape=jax.ShapeDtypeStruct((clips, rows, width), jnp.bfloat16),
        cost_estimate=cost(clips * rows * width * WIDTH, 2 * (width * WIDTH + 3 * clips * rows * width), 0),
        compiler_params=pltpu.CompilerParams(vmem_limit_bytes=VMEM_LIMIT),
        name="final",
    )(mixed, context, time_output)


def per_device(video_in, space_gain, space_project, space_output, time_gain, time_project, time_output):
    clip_count, frame_local, patch_count, width = video_in.shape
    count = lax.axis_size("grp") * lax.axis_size("dev")
    patch_here = patch_count // count
    video = video_in.reshape(clip_count, patch_count, width)
    gains = space_gain.reshape(1, width), time_gain.reshape(1, width)
    mixed, arrived, returned = [], [], []
    first = 0
    for clips in CHUNKS:
        here, sent = space_call(video, first, clips, gains[0], space_project, space_output, gains[1], count)
        mixed.append(here)
        arrived.append(exchange(sent, count, patch_here))
        first += clips
    for clips, rows in zip(CHUNKS, arrived):
        context = time_call(rows, clips, patch_count, time_project, count)
        returned.append(exchange(context, count, patch_here))
    done = [final_call(here, context, time_output, count) for here, context in zip(mixed, returned)]
    return jnp.concatenate(done, axis=0).reshape(clip_count, frame_local, patch_count, width)


def solution(mesh):
    in_specs = (P(None, AXES, None, None), P(), P(), P(), P(), P(), P())
    return jax.shard_map(
        per_device, mesh=mesh, in_specs=in_specs, out_specs=P(None, AXES, None, None), check_vma=False
    )
```

```python
from functools import partial

import jax
import jax.numpy as jnp
from jax import lax
from jax.experimental import pallas as pl
from jax.experimental.pallas import tpu as pltpu
from jax.sharding import PartitionSpec as P

HEADS = 8
HEAD_DIM = 64
WIDTH = HEADS * HEAD_DIM
LANES = 128
EPSILON = 1e-06
MASKED = -1e30
ANYWHERE = pl.BlockSpec(memory_space=pl.ANY)
AXES = ("grp", "dev")
VMEM_LIMIT = 60 * 1024 * 1024
TIME_VMEM_LIMIT = 40 * 1024 * 1024
FINAL_VMEM_LIMIT = 40 * 1024 * 1024


def normed(floats, gain):
    centred = floats - jnp.mean(floats, axis=-1, keepdims=True)
    spread = jnp.mean(jnp.square(centred), axis=-1, keepdims=True)
    return centred * lax.rsqrt(spread + EPSILON) * gain


def attend(heads, bias):
    rows = heads.shape[0]
    low = lax.broadcasted_iota(jnp.int32, (rows, LANES), 1) < HEAD_DIM
    ones = jnp.ones((rows, LANES), jnp.bfloat16)
    contexts, pending = [], []
    for pair in range(WIDTH // LANES):
        at = pair * LANES
        queries = heads[:, at : at + LANES] * jnp.bfloat16(HEAD_DIM**-0.5)
        keys = heads[:, WIDTH + at : WIDTH + at + LANES]
        values = heads[:, 2 * WIDTH + at : 2 * WIDTH + at + LANES]
        nothing = jnp.zeros_like(queries)
        stacked = jnp.concatenate([jnp.where(low, queries, nothing), jnp.where(low, nothing, queries)], axis=0)
        scores = lax.dot_general(stacked, keys, (((1,), (1,)), ((), ())), preferred_element_type=jnp.float32)
        if bias is not None:
            scores = scores + jnp.concatenate([bias, bias], axis=0)
        weights = jnp.exp(scores - jnp.max(scores, axis=-1, keepdims=True)).astype(jnp.bfloat16)
        pending.append((weights, values))
    for weights, values in pending:
        sums = jnp.dot(weights, jnp.concatenate([values, ones], axis=1), preferred_element_type=jnp.float32)
        context = sums[:, :LANES] / sums[:, LANES:]
        contexts.append(jnp.where(low, context[:rows], context[rows:]))
    return jnp.concatenate(contexts, axis=1).astype(jnp.bfloat16)


def bit_groups():
    inner = lax.axis_size("dev").bit_length() - 1
    bits = inner + lax.axis_size("grp").bit_length() - 1
    far = [tuple(reversed(range(1, inner)))]
    near = [(0,), *((bit,) for bit in reversed(range(inner, bits)))]
    return near + far


def mask_of(index, group):
    return sum(((index >> (len(group) - 1 - at)) & 1) << bit for at, bit in enumerate(group))


def put(parts, scratch, out_refs, groups):
    if groups is None:
        out_refs[0][...] = parts.reshape(out_refs[0].shape)
        return
    scratch[...] = parts
    me = lax.axis_index(AXES)
    order = sum(groups, ())
    size = out_refs[0].shape[0]
    for place in range(size * len(out_refs)):
        out_refs[place // size][place % size, 0] = scratch[mask_of(place, order) ^ me]


def take(ref, groups):
    if groups is None:
        return ref[...]
    me = lax.axis_index(AXES)
    order = sum(groups, ())
    parts = []
    for device in range(ref.shape[0]):
        slot = device ^ me
        place = sum(((slot >> bit) & 1) << (len(order) - 1 - at) for at, bit in enumerate(order))
        parts.append(ref[place, 0])
    return jnp.stack(parts)


def space_kernel(video_ref, gain_ref, project_ref, output_ref, time_gain_ref, *refs):
    mixed_ref, sent_ref = refs[-2:]
    floats = video_ref[0].astype(jnp.float32)
    heads = jnp.dot(
        normed(floats, gain_ref[...]).astype(jnp.bfloat16), project_ref[...], preferred_element_type=jnp.float32
    ).astype(jnp.bfloat16)
    context = attend(heads, None)
    mixed = (floats + jnp.dot(context, output_ref[...], preferred_element_type=jnp.float32)).astype(jnp.bfloat16)
    mixed_ref[0] = mixed
    sent = normed(mixed.astype(jnp.float32), time_gain_ref[...])
    sent_ref[...] = sent.reshape(sent_ref.shape).astype(jnp.bfloat16)


def time_kernel(back, extra, patch_here, rows_ref, project_ref, *refs):
    *context_refs, bias_ref = refs[extra:]
    context_refs, scratch = (context_refs, None) if back is None else (context_refs[:-1], context_refs[-1])
    rows, width = bias_ref.shape[0], rows_ref.shape[-1]

    @pl.when(pl.program_id(0) == 0)
    def _():
        query = lax.broadcasted_iota(jnp.int32, (rows, rows), 0)
        key = lax.broadcasted_iota(jnp.int32, (rows, rows), 1)
        seen = (key <= query) & (lax.rem(query, patch_here) == lax.rem(key, patch_here))
        bias_ref[...] = jnp.where(seen, 0.0, MASKED)

    arrived = rows_ref[...].astype(jnp.float32).reshape(rows, width).astype(jnp.bfloat16)
    heads = jnp.dot(arrived, project_ref[...], preferred_element_type=jnp.float32).astype(jnp.bfloat16)
    context = attend(heads, bias_ref[...]).astype(jnp.float32)
    shape = context_refs[0].shape if back is None else scratch.shape
    put(context.reshape(shape).astype(jnp.bfloat16), scratch, context_refs, back)


def final_kernel(order, mixed_ref, context_ref, output_ref, *refs):
    out_ref = refs[-1]
    rows = mixed_ref.shape[1]
    context = take(context_ref, order).astype(jnp.float32).reshape(rows, WIDTH).astype(jnp.bfloat16)
    update = jnp.dot(context, output_ref[...], preferred_element_type=jnp.float32)
    out_ref[0] = (mixed_ref[0].astype(jnp.float32) + update).astype(jnp.bfloat16)


def whole(shape):
    return pl.BlockSpec(shape, lambda c: (0,) * len(shape))


def exchange_spec(count, patch_here, width):
    if patch_here % 8:
        return pl.BlockSpec((1, count * patch_here, width), lambda c: (c, 0, 0))
    return pl.BlockSpec((count, 1, patch_here, width), lambda c: (0, c, 0, 0))


def exchange_shape(count, clips, patch_here, width):
    if patch_here % 8:
        return jax.ShapeDtypeStruct((clips, count * patch_here, width), jnp.bfloat16)
    return jax.ShapeDtypeStruct((count, clips, patch_here, width), jnp.bfloat16)


def exchange(sent, count, patch_here):
    plain = sent.ndim == 3
    if plain:
        clips, _, width = sent.shape
        sent = sent.reshape(clips, count, patch_here, width).transpose(1, 0, 2, 3)
    arrived = lax.all_to_all(sent, AXES, split_axis=0, concat_axis=0, tiled=True)
    if plain:
        arrived = arrived.transpose(1, 0, 2, 3).reshape(clips, count * patch_here, width)
    return arrived


def in_hbm(array):
    return pltpu.with_memory_space_constraint(array, pltpu.HBM)


def after(rows, awaited):
    return pl.pallas_call(
        lambda *refs: None,
        in_specs=[ANYWHERE] * (1 + len(awaited)),
        out_specs=ANYWHERE,
        out_shape=jax.ShapeDtypeStruct(rows.shape, rows.dtype),
        input_output_aliases={0: 0},
        compiler_params=pltpu.CompilerParams(vmem_limit_bytes=2 * 1024 * 1024),
        name="after",
    )(rows, *awaited)


def swap(blocks, groups):
    devices = 1 << len(sum(groups, ()))
    rows = blocks[0].shape[1:]
    blocks = [block.reshape(1, *(1 << len(group) for group in groups[1:]), *rows) for block in blocks]
    for at, group in enumerate(groups):
        arrived = [
            lax.ppermute(block, AXES, [(device, device ^ mask_of(index, group)) for device in range(devices)])
            for index, block in enumerate(blocks)
            if index
        ]
        if len(group) > 1:
            awaited = arrived
        whole_buffer = jnp.concatenate([blocks[0], *arrived], axis=at)
        if at + 1 < len(groups):
            blocks = jnp.split(whole_buffer, 1 << len(groups[at + 1]), axis=at + 1)
    return whole_buffer.reshape(devices, *rows), awaited


def cost(macs, bytes_accessed, exps):
    return pl.CostEstimate(flops=2 * macs, bytes_accessed=bytes_accessed, transcendentals=exps)


def sent_specs(count, clips, patch_here, width, order):
    if order is None:
        return [exchange_shape(count, clips, patch_here, width)], [exchange_spec(count, patch_here, width)], []
    parts = 1 << len(order[0])
    shape = exchange_shape(count // parts, clips, patch_here, width)
    spec = exchange_spec(count // parts, patch_here, width)
    return [shape] * parts, [spec] * parts, [pltpu.VMEM((count, patch_here, width), jnp.bfloat16)]


def space_call(video, first, clips, space_gain, space_project, space_output, time_gain, count, before):
    rows, width = video.shape[1:]
    return pl.pallas_call(
        space_kernel,
        grid=(clips,),
        in_specs=[
            pl.BlockSpec((1, rows, width), lambda c: (first + c, 0, 0)),
            whole((1, width)),
            whole((width, 3 * WIDTH)),
            whole((WIDTH, width)),
            whole((1, width)),
        ]
        + [ANYWHERE] * len(before),
        out_specs=[pl.BlockSpec((1, rows, width), lambda c: (c, 0, 0)), exchange_spec(count, rows // count, width)],
        out_shape=[jax.ShapeDtypeStruct((clips, rows, width), jnp.bfloat16), exchange_shape(count, clips, rows // count, width)],
        cost_estimate=cost(
            clips * rows * (width * 4 * WIDTH + 8 * rows * WIDTH), 2 * (4 * width * WIDTH + 3 * clips * rows * width),
            clips * HEADS * rows * rows,
        ),
        compiler_params=pltpu.CompilerParams(vmem_limit_bytes=VMEM_LIMIT),
        name="space",
    )(video, space_gain, space_project, space_output, time_gain, *map(in_hbm, before))


def time_call(arrived, clips, rows, time_project, count, before, back):
    width = arrived.shape[-1]
    patch_here = rows // count
    shapes, specs, scratch = sent_specs(count, clips, patch_here, WIDTH, back)
    return pl.pallas_call(
        partial(time_kernel, back, len(before), patch_here),
        grid=(clips,),
        in_specs=[exchange_spec(count, patch_here, width), whole((width, 3 * WIDTH))] + [ANYWHERE] * len(before),
        out_specs=specs,
        out_shape=shapes,
        scratch_shapes=scratch + [pltpu.VMEM((rows, rows), jnp.float32)],
        cost_estimate=cost(
            clips * rows * (width * 3 * WIDTH + 8 * rows * WIDTH), 2 * (3 * width * WIDTH + 2 * clips * rows * width),
            clips * HEADS * rows * rows,
        ),
        compiler_params=pltpu.CompilerParams(vmem_limit_bytes=TIME_VMEM_LIMIT),
        name="time",
    )(arrived, in_hbm(time_project), *map(in_hbm, before))


def final_call(mixed, context, time_output, count, first, total, before, order):
    clips, rows, width = mixed.shape
    return pl.pallas_call(
        partial(final_kernel, order),
        grid=(clips,),
        in_specs=[
            pl.BlockSpec((1, rows, width), lambda c: (c, 0, 0)),
            exchange_spec(count, rows // count, WIDTH),
            whole((WIDTH, width)),
        ]
        + [ANYWHERE] * len(before),
        out_specs=pl.BlockSpec((1, rows, width), lambda c: (first + c, 0, 0)),
        out_shape=jax.ShapeDtypeStruct((total, rows, width), jnp.bfloat16),
        input_output_aliases={3: 0} if before else {},
        cost_estimate=cost(clips * rows * width * WIDTH, 2 * (width * WIDTH + 3 * clips * rows * width), 0),
        compiler_params=pltpu.CompilerParams(vmem_limit_bytes=FINAL_VMEM_LIMIT),
        name="final",
    )(mixed, context, time_output, *before)


def per_device(video_in, space_gain, space_project, space_output, time_gain, time_project, time_output):
    clip_count, frame_local, patch_count, width = video_in.shape
    count = lax.axis_size("grp") * lax.axis_size("dev")
    patch_here = patch_count // count
    video = video_in.reshape(clip_count, patch_count, width)
    weights = space_gain.reshape(1, width), space_project, space_output, time_gain.reshape(1, width)
    swappable = patch_here % 8 == 0 and count & (count - 1) == 0
    back = bit_groups() if swappable else None
    chunks = [(0, 1), (1, clip_count - 1)]
    mixed, arrived, out = [], [], []
    for first, clips in chunks:
        kept, sent = space_call(video, first, clips, *weights, count, mixed)
        mixed.append(kept)
        arrived.append(exchange(sent, count, patch_here))
    context = time_call(arrived[0], 1, patch_count, time_project, count, [], back)
    if swappable:
        early, awaited = swap(context, back)
    else:
        early, awaited = exchange(context[0], count, patch_here), []
    context = time_call(arrived[1], clip_count - 1, patch_count, time_project, count, context[:1], None)
    late = exchange(after(context[0], awaited) if awaited else context[0], count, patch_here)
    for (first, _), kept, context, groups in zip(chunks, mixed, (early, late), (back, None)):
        out = [final_call(kept, context, time_output, count, first, clip_count, out, groups)]
    return out[0].reshape(clip_count, frame_local, patch_count, width)


def solution(mesh):
    in_specs = (P(None, AXES, None, None), P(), P(), P(), P(), P(), P())
    return jax.shard_map(
        per_device, mesh=mesh, in_specs=in_specs, out_specs=P(None, AXES, None, None), check_vma=False
    )
```

```python
from functools import partial

import jax
import jax.numpy as jnp
from jax import lax
from jax.experimental import pallas as pl
from jax.experimental.pallas import tpu as pltpu
from jax.sharding import PartitionSpec as P

HEADS = 8
HEAD_DIM = 64
WIDTH = HEADS * HEAD_DIM
LANES = 128
EPSILON = 1e-06
MASKED = -1e30
SPLIT = 2
PIECES = 3
ANYWHERE = pl.BlockSpec(memory_space=pl.ANY)
AXES = ("grp", "dev")
VMEM_LIMIT = 60 * 1024 * 1024
TIME_VMEM_LIMIT = 40 * 1024 * 1024
FINAL_VMEM_LIMIT = 40 * 1024 * 1024


def normed(floats, gain):
    centred = floats - jnp.mean(floats, axis=-1, keepdims=True)
    spread = jnp.mean(jnp.square(centred), axis=-1, keepdims=True)
    return centred * lax.rsqrt(spread + EPSILON) * gain


def attend(heads, bias):
    rows = heads.shape[0]
    low = lax.broadcasted_iota(jnp.int32, (rows, LANES), 1) < HEAD_DIM
    ones = jnp.ones((rows, LANES), jnp.bfloat16)
    contexts, pending = [], []
    for pair in range(WIDTH // LANES):
        at = pair * LANES
        queries = heads[:, at : at + LANES] * jnp.bfloat16(HEAD_DIM**-0.5)
        keys = heads[:, WIDTH + at : WIDTH + at + LANES]
        values = heads[:, 2 * WIDTH + at : 2 * WIDTH + at + LANES]
        nothing = jnp.zeros_like(queries)
        stacked = jnp.concatenate([jnp.where(low, queries, nothing), jnp.where(low, nothing, queries)], axis=0)
        scores = lax.dot_general(stacked, keys, (((1,), (1,)), ((), ())), preferred_element_type=jnp.float32)
        if bias is not None:
            scores = scores + jnp.concatenate([bias, bias], axis=0)
        weights = jnp.exp(scores - jnp.max(scores, axis=-1, keepdims=True)).astype(jnp.bfloat16)
        pending.append((weights, values))
    for weights, values in pending:
        sums = jnp.dot(weights, jnp.concatenate([values, ones], axis=1), preferred_element_type=jnp.float32)
        context = sums[:, :LANES] / sums[:, LANES:]
        contexts.append(jnp.where(low, context[:rows], context[rows:]))
    return jnp.concatenate(contexts, axis=1).astype(jnp.bfloat16)


def bit_groups():
    inner = lax.axis_size("dev").bit_length() - 1
    bits = inner + lax.axis_size("grp").bit_length() - 1
    return [(inner,), (0, *reversed(range(inner + 1, bits))), tuple(reversed(range(1, inner)))]


def mask_of(index, group):
    return sum(((index >> (len(group) - 1 - at)) & 1) << bit for at, bit in enumerate(group))


def put(parts, scratch, out_refs, groups):
    if groups is None:
        out_refs[0][...] = parts.reshape(out_refs[0].shape)
        return
    scratch[...] = parts
    me = lax.axis_index(AXES)
    order = sum(groups, ())
    size = out_refs[0].shape[0]
    for place in range(size * len(out_refs)):
        out_refs[place // size][place % size, 0] = scratch[mask_of(place, order) ^ me]


def take(ref, groups):
    if groups is None:
        return ref[...]
    me = lax.axis_index(AXES)
    order = sum(groups, ())
    parts = []
    for device in range(ref.shape[0]):
        slot = device ^ me
        place = sum(((slot >> bit) & 1) << (len(order) - 1 - at) for at, bit in enumerate(order))
        parts.append(ref[place, 0])
    return jnp.stack(parts)


def space_kernel(groups, extra, video_ref, gain_ref, project_ref, output_ref, time_gain_ref, *refs):
    mixed_ref, *sent_refs = refs[extra:]
    sent_refs, scratch = (sent_refs, None) if groups is None else (sent_refs[:-1], sent_refs[-1])
    floats = video_ref[0].astype(jnp.float32)
    heads = jnp.dot(
        normed(floats, gain_ref[...]).astype(jnp.bfloat16), project_ref[...], preferred_element_type=jnp.float32
    ).astype(jnp.bfloat16)
    context = attend(heads, None)
    mixed = (floats + jnp.dot(context, output_ref[...], preferred_element_type=jnp.float32)).astype(jnp.bfloat16)
    mixed_ref[0] = mixed
    sent = normed(mixed.astype(jnp.float32), time_gain_ref[...])
    shape = sent_refs[0].shape if groups is None else scratch.shape
    put(sent.reshape(shape).astype(jnp.bfloat16), scratch, sent_refs, groups)


def time_kernel(groups, back, extra, patch_here, rows_ref, project_ref, *refs):
    *context_refs, bias_ref = refs[extra:]
    context_refs, scratch = (context_refs, None) if back is None else (context_refs[:-1], context_refs[-1])
    rows, width = bias_ref.shape[0], rows_ref.shape[-1]

    @pl.when(pl.program_id(0) == 0)
    def _():
        query = lax.broadcasted_iota(jnp.int32, (rows, rows), 0)
        key = lax.broadcasted_iota(jnp.int32, (rows, rows), 1)
        seen = (key <= query) & (lax.rem(query, patch_here) == lax.rem(key, patch_here))
        bias_ref[...] = jnp.where(seen, 0.0, MASKED)

    arrived = take(rows_ref, groups).astype(jnp.float32).reshape(rows, width).astype(jnp.bfloat16)
    heads = jnp.dot(arrived, project_ref[...], preferred_element_type=jnp.float32).astype(jnp.bfloat16)
    context = attend(heads, bias_ref[...]).astype(jnp.float32)
    shape = context_refs[0].shape if back is None else scratch.shape
    put(context.reshape(shape).astype(jnp.bfloat16), scratch, context_refs, back)


def time_wide_kernel(
    patch_here, rows_ref, project_ref, before_ref, context_ref, bias_ref, project, heads, contexts, weight_sems, out_sems
):
    clips, rows, width = heads.shape[0], bias_ref.shape[0], rows_ref.shape[-1]
    tile = heads.shape[2] // weight_sems.shape[0]

    def columns(piece):
        return pl.ds(piece * tile, tile)

    def leaving(clip):
        return pltpu.make_async_copy(contexts.at[clip], context_ref.at[:, clip], out_sems.at[clip])

    weights = [
        pltpu.make_async_copy(project_ref.at[:, columns(piece)], project.at[:, columns(piece)], weight_sems.at[piece])
        for piece in range(weight_sems.shape[0])
    ]
    for copy in weights:
        copy.start()
    query = lax.broadcasted_iota(jnp.int32, (rows, rows), 0)
    key = lax.broadcasted_iota(jnp.int32, (rows, rows), 1)
    seen = (key <= query) & (lax.rem(query, patch_here) == lax.rem(key, patch_here))
    bias_ref[...] = jnp.where(seen, 0.0, MASKED)
    arrived = [rows_ref[:, clip].astype(jnp.float32).reshape(rows, width).astype(jnp.bfloat16) for clip in range(clips)]
    for piece, copy in enumerate(weights):
        copy.wait()
        for at, one in enumerate(arrived):
            got = jnp.dot(one, project[:, columns(piece)], preferred_element_type=jnp.float32).astype(jnp.bfloat16)
            heads[at, :, columns(piece)] = got
    for clip in range(clips):
        context = attend(heads[clip], bias_ref[...])
        contexts[clip] = context.astype(jnp.float32).reshape(contexts.shape[1:]).astype(jnp.bfloat16)
        leaving(clip).start()
    for clip in range(clips):
        leaving(clip).wait()


def final_kernel(order, mixed_ref, context_ref, output_ref, *refs):
    out_ref = refs[-1]
    rows = mixed_ref.shape[1]
    context = take(context_ref, order).astype(jnp.float32).reshape(rows, WIDTH).astype(jnp.bfloat16)
    update = jnp.dot(context, output_ref[...], preferred_element_type=jnp.float32)
    out_ref[0] = (mixed_ref[0].astype(jnp.float32) + update).astype(jnp.bfloat16)


def final_wide_kernel(first, mixed_ref, context_ref, output_ref, before_ref, out_ref, done, sems):
    clips, rows, _ = mixed_ref.shape
    part = rows // SPLIT
    copies = []
    for clip in range(clips):
        context = context_ref[:, clip].astype(jnp.float32).reshape(rows, WIDTH).astype(jnp.bfloat16)
        for at in range(SPLIT):
            here = slice(at * part, (at + 1) * part)
            update = jnp.dot(context[here], output_ref[...], preferred_element_type=jnp.float32)
            done[clip, here] = (mixed_ref[clip, here].astype(jnp.float32) + update).astype(jnp.bfloat16)
            copies.append(
                pltpu.make_async_copy(
                    done.at[clip, pl.ds(at * part, part)],
                    out_ref.at[first + clip, pl.ds(at * part, part)],
                    sems.at[clip, at],
                )
            )
            copies[-1].start()
    for copy in copies:
        copy.wait()


def whole(shape):
    return pl.BlockSpec(shape, lambda c: (0,) * len(shape))


def exchange_spec(count, patch_here, width):
    if patch_here % 8:
        return pl.BlockSpec((1, count * patch_here, width), lambda c: (c, 0, 0))
    return pl.BlockSpec((count, 1, patch_here, width), lambda c: (0, c, 0, 0))


def exchange_shape(count, clips, patch_here, width):
    if patch_here % 8:
        return jax.ShapeDtypeStruct((clips, count * patch_here, width), jnp.bfloat16)
    return jax.ShapeDtypeStruct((count, clips, patch_here, width), jnp.bfloat16)


def exchange(sent, count, patch_here):
    plain = sent.ndim == 3
    if plain:
        clips, _, width = sent.shape
        sent = sent.reshape(clips, count, patch_here, width).transpose(1, 0, 2, 3)
    arrived = lax.all_to_all(sent, AXES, split_axis=0, concat_axis=0, tiled=True)
    if plain:
        arrived = arrived.transpose(1, 0, 2, 3).reshape(clips, count * patch_here, width)
    return arrived


def in_hbm(array):
    return pltpu.with_memory_space_constraint(array, pltpu.HBM)


def after(rows, awaited):
    return pl.pallas_call(
        lambda *refs: None,
        in_specs=[ANYWHERE] * (1 + len(awaited)),
        out_specs=ANYWHERE,
        out_shape=jax.ShapeDtypeStruct(rows.shape, rows.dtype),
        input_output_aliases={0: 0},
        compiler_params=pltpu.CompilerParams(vmem_limit_bytes=2 * 1024 * 1024),
        name="after",
    )(in_hbm(rows), *awaited)


def swap(blocks, groups):
    steps = []
    devices = 1 << len(sum(groups, ()))
    rows = blocks[0].shape[1:]
    blocks = [block.reshape(1, *(1 << len(group) for group in groups[1:]), *rows) for block in blocks]
    for at, group in enumerate(groups):
        arrived = [
            lax.ppermute(block, AXES, [(device, device ^ mask_of(index, group)) for device in range(devices)])
            for index, block in enumerate(blocks)
            if index
        ]
        steps.append(arrived)
        whole_buffer = jnp.concatenate([blocks[0], *arrived], axis=at)
        if at + 1 < len(groups):
            blocks = jnp.split(whole_buffer, 1 << len(groups[at + 1]), axis=at + 1)
    return whole_buffer.reshape(devices, *rows), steps


def cost(macs, bytes_accessed, exps):
    return pl.CostEstimate(flops=2 * macs, bytes_accessed=bytes_accessed, transcendentals=exps)


def sent_specs(count, clips, patch_here, width, order):
    if order is None:
        return [exchange_shape(count, clips, patch_here, width)], [exchange_spec(count, patch_here, width)], []
    parts = 1 << len(order[0])
    shape = exchange_shape(count // parts, clips, patch_here, width)
    spec = exchange_spec(count // parts, patch_here, width)
    return [shape] * parts, [spec] * parts, [pltpu.VMEM((count, patch_here, width), jnp.bfloat16)]


def space_call(video, first, clips, space_gain, space_project, space_output, time_gain, count, before, groups):
    rows, width = video.shape[1:]
    shapes, specs, scratch = sent_specs(count, clips, rows // count, width, groups)
    mixed, *sent = pl.pallas_call(
        partial(space_kernel, groups, len(before)),
        grid=(clips,),
        in_specs=[
            pl.BlockSpec((1, rows, width), lambda c: (first + c, 0, 0)),
            whole((1, width)),
            whole((width, 3 * WIDTH)),
            whole((WIDTH, width)),
            whole((1, width)),
        ]
        + [ANYWHERE] * len(before),
        out_specs=[pl.BlockSpec((1, rows, width), lambda c: (c, 0, 0)), *specs],
        out_shape=[jax.ShapeDtypeStruct((clips, rows, width), jnp.bfloat16), *shapes],
        scratch_shapes=scratch,
        cost_estimate=cost(
            clips * rows * (width * 4 * WIDTH + 8 * rows * WIDTH), 2 * (4 * width * WIDTH + 3 * clips * rows * width),
            clips * HEADS * rows * rows,
        ),
        compiler_params=pltpu.CompilerParams(vmem_limit_bytes=VMEM_LIMIT),
        name="space",
    )(video, space_gain, space_project, space_output, time_gain, *map(in_hbm, before))
    return mixed, sent


def time_call(arrived, clips, rows, time_project, count, before, groups, back):
    width = arrived.shape[-1]
    patch_here = rows // count
    shapes, specs, scratch = sent_specs(count, clips, patch_here, WIDTH, back)
    return pl.pallas_call(
        partial(time_kernel, groups, back, len(before), patch_here),
        grid=(clips,),
        in_specs=[exchange_spec(count, patch_here, width), whole((width, 3 * WIDTH))] + [ANYWHERE] * len(before),
        out_specs=specs,
        out_shape=shapes,
        scratch_shapes=scratch + [pltpu.VMEM((rows, rows), jnp.float32)],
        cost_estimate=cost(
            clips * rows * (width * 3 * WIDTH + 8 * rows * WIDTH), 2 * (3 * width * WIDTH + 2 * clips * rows * width),
            clips * HEADS * rows * rows,
        ),
        compiler_params=pltpu.CompilerParams(vmem_limit_bytes=TIME_VMEM_LIMIT),
        name="time",
    )(arrived, in_hbm(time_project), *map(in_hbm, before))


def time_wide_call(arrived, clips, rows, time_project, count, before):
    width = arrived.shape[-1]
    patch_here = rows // count
    return pl.pallas_call(
        partial(time_wide_kernel, patch_here),
        in_specs=[pl.BlockSpec(memory_space=pltpu.VMEM), ANYWHERE, ANYWHERE],
        out_specs=ANYWHERE,
        out_shape=pltpu.HBM((count, clips, patch_here, WIDTH), jnp.bfloat16),
        scratch_shapes=[
            pltpu.VMEM((rows, rows), jnp.float32),
            pltpu.VMEM((width, 3 * WIDTH), jnp.bfloat16),
            pltpu.VMEM((clips, rows, 3 * WIDTH), jnp.bfloat16),
            pltpu.VMEM((clips, count, patch_here, WIDTH), jnp.bfloat16),
            pltpu.SemaphoreType.DMA((PIECES,)),
            pltpu.SemaphoreType.DMA((clips,)),
        ],
        cost_estimate=cost(
            clips * rows * (width * 3 * WIDTH + 8 * rows * WIDTH), 2 * (3 * width * WIDTH + 2 * clips * rows * width),
            clips * HEADS * rows * rows,
        ),
        compiler_params=pltpu.CompilerParams(vmem_limit_bytes=TIME_VMEM_LIMIT),
        name="time",
    )(arrived, in_hbm(time_project), in_hbm(before))


def final_call(mixed, context, time_output, count, first, total, before, order):
    clips, rows, width = mixed.shape
    return pl.pallas_call(
        partial(final_kernel, order),
        grid=(clips,),
        in_specs=[
            pl.BlockSpec((1, rows, width), lambda c: (c, 0, 0)),
            exchange_spec(count, rows // count, WIDTH),
            whole((WIDTH, width)),
        ]
        + [ANYWHERE] * len(before),
        out_specs=pl.BlockSpec((1, rows, width), lambda c: (first + c, 0, 0)),
        out_shape=jax.ShapeDtypeStruct((total, rows, width), jnp.bfloat16),
        input_output_aliases={3: 0} if before else {},
        cost_estimate=cost(clips * rows * width * WIDTH, 2 * (width * WIDTH + 3 * clips * rows * width), 0),
        compiler_params=pltpu.CompilerParams(vmem_limit_bytes=FINAL_VMEM_LIMIT),
        name="final",
    )(mixed, context, time_output, *before)


def final_wide_call(mixed, context, time_output, first, total, before):
    clips, rows, width = mixed.shape
    vmem = pl.BlockSpec(memory_space=pltpu.VMEM)
    return pl.pallas_call(
        partial(final_wide_kernel, first),
        in_specs=[vmem, vmem, vmem, ANYWHERE],
        out_specs=ANYWHERE,
        out_shape=jax.ShapeDtypeStruct((total, rows, width), jnp.bfloat16),
        scratch_shapes=[pltpu.VMEM((clips, rows, width), jnp.bfloat16), pltpu.SemaphoreType.DMA((clips, SPLIT))],
        input_output_aliases={3: 0},
        cost_estimate=cost(clips * rows * width * WIDTH, 2 * (width * WIDTH + 3 * clips * rows * width), 0),
        compiler_params=pltpu.CompilerParams(vmem_limit_bytes=FINAL_VMEM_LIMIT),
        name="final",
    )(mixed, context, time_output, before)


def per_device(video_in, space_gain, space_project, space_output, time_gain, time_project, time_output):
    clip_count, frame_local, patch_count, width = video_in.shape
    count = lax.axis_size("grp") * lax.axis_size("dev")
    patch_here = patch_count // count
    video = video_in.reshape(clip_count, patch_count, width)
    weights = space_gain.reshape(1, width), space_project, space_output, time_gain.reshape(1, width)
    swappable = patch_here % 8 == 0 and count & (count - 1) == 0
    if not swappable:
        return plainly(video, weights, time_project, time_output, count).reshape(video_in.shape)
    others = clip_count - 1
    back = bit_groups()
    there = [back[2], back[0], back[1]]
    kept, sent = space_call(video, 0, 1, *weights, count, [], there)
    kept_others, sent_others = space_call(video, 1, others, *weights, count, [kept], None)
    arrived, steps = swap(sent, there)
    arrived_others = exchange(after(sent_others[0], steps[0]), count, patch_here)
    context = time_call(arrived, 1, patch_count, time_project, count, [], there, back)
    returned, steps = swap(context, back)
    context = time_wide_call(arrived_others, others, patch_count, time_project, count, context[0])
    returned_others = exchange(after(context, steps[-1]), count, patch_here)
    out = final_call(kept, returned, time_output, count, 0, clip_count, [], back)
    out = final_wide_call(kept_others, returned_others, time_output, 1, clip_count, out)
    return out.reshape(clip_count, frame_local, patch_count, width)


def plainly(video, weights, time_project, time_output, count):
    clips, rows, _ = video.shape
    kept, sent = space_call(video, 0, clips, *weights, count, [], None)
    arrived = exchange(sent[0], count, rows // count)
    context = time_call(arrived, clips, rows, time_project, count, [], None, None)
    returned = exchange(context[0], count, rows // count)
    return final_call(kept, returned, time_output, count, 0, clips, [], None)


def solution(mesh):
    in_specs = (P(None, AXES, None, None), P(), P(), P(), P(), P(), P())
    return jax.shard_map(
        per_device, mesh=mesh, in_specs=in_specs, out_specs=P(None, AXES, None, None), check_vma=False
    )
```

```python
from functools import partial

import jax
import jax.numpy as jnp
from jax import lax
from jax.experimental import pallas as pl
from jax.experimental.pallas import tpu as pltpu
from jax.sharding import PartitionSpec as P

HEADS = 8
HEAD_DIM = 64
WIDTH = HEADS * HEAD_DIM
LANES = 128
EPSILON = 1e-06
MASKED = -1e30
SPACE_VMEM_LIMIT = 40 * 1024 * 1024
SPLIT = 2
PIECES = 3
ANYWHERE = pl.BlockSpec(memory_space=pl.ANY)
AXES = ("grp", "dev")
VMEM_LIMIT = 60 * 1024 * 1024
TIME_VMEM_LIMIT = 40 * 1024 * 1024
FINAL_VMEM_LIMIT = 40 * 1024 * 1024


def normed(floats, gain):
    centred = floats - jnp.mean(floats, axis=-1, keepdims=True)
    spread = jnp.mean(jnp.square(centred), axis=-1, keepdims=True)
    return centred * lax.rsqrt(spread + EPSILON) * gain


def attend(heads, bias):
    rows = heads.shape[0]
    low = lax.broadcasted_iota(jnp.int32, (rows, LANES), 1) < HEAD_DIM
    ones = jnp.ones((rows, LANES), jnp.bfloat16)
    contexts, pending = [], []
    for pair in range(WIDTH // LANES):
        at = pair * LANES
        queries = heads[:, at : at + LANES] * jnp.bfloat16(HEAD_DIM**-0.5)
        keys = heads[:, WIDTH + at : WIDTH + at + LANES]
        values = heads[:, 2 * WIDTH + at : 2 * WIDTH + at + LANES]
        nothing = jnp.zeros_like(queries)
        stacked = jnp.concatenate([jnp.where(low, queries, nothing), jnp.where(low, nothing, queries)], axis=0)
        scores = lax.dot_general(stacked, keys, (((1,), (1,)), ((), ())), preferred_element_type=jnp.float32)
        if bias is not None:
            scores = scores + jnp.concatenate([bias, bias], axis=0)
        weights = jnp.exp(scores - jnp.max(scores, axis=-1, keepdims=True)).astype(jnp.bfloat16)
        pending.append((weights, values))
    for weights, values in pending:
        sums = jnp.dot(weights, jnp.concatenate([values, ones], axis=1), preferred_element_type=jnp.float32)
        context = sums[:, :LANES] / sums[:, LANES:]
        contexts.append(jnp.where(low, context[:rows], context[rows:]))
    return jnp.concatenate(contexts, axis=1).astype(jnp.bfloat16)


def bit_groups():
    inner = lax.axis_size("dev").bit_length() - 1
    bits = inner + lax.axis_size("grp").bit_length() - 1
    return [(inner,), (0, *reversed(range(inner + 1, bits))), tuple(reversed(range(1, inner)))]


def mask_of(index, group):
    return sum(((index >> (len(group) - 1 - at)) & 1) << bit for at, bit in enumerate(group))


def put(parts, scratch, out_refs, groups):
    if groups is None:
        out_refs[0][...] = parts.reshape(out_refs[0].shape)
        return
    scratch[...] = parts
    me = lax.axis_index(AXES)
    order = sum(groups, ())
    size = out_refs[0].shape[0]
    for place in range(size * len(out_refs)):
        out_refs[place // size][place % size, 0] = scratch[mask_of(place, order) ^ me]


def take(ref, groups):
    if groups is None:
        return ref[...]
    me = lax.axis_index(AXES)
    order = sum(groups, ())
    parts = []
    for device in range(ref.shape[0]):
        slot = device ^ me
        place = sum(((slot >> bit) & 1) << (len(order) - 1 - at) for at, bit in enumerate(order))
        parts.append(ref[place, 0])
    return jnp.stack(parts)


def space_first_kernel(
    groups, video_ref, gain_ref, project_ref, output_ref, time_gain_ref, mixed_ref, project, output, *refs
):
    *sent_refs, frame, gains, mixed, scratch, sems = refs
    parts = sent_refs[0].shape[0]
    frame_copy = pltpu.make_async_copy(video_ref.at[0], frame, sems.at[0])
    gain_copy = pltpu.make_async_copy(gain_ref, gains.at[pl.ds(0, 1)], sems.at[1])
    weight_copies = [
        pltpu.make_async_copy(project_ref, project, sems.at[2]),
        pltpu.make_async_copy(output_ref, output, sems.at[3]),
        pltpu.make_async_copy(time_gain_ref, gains.at[pl.ds(1, 1)], sems.at[4]),
    ]
    mixed_copy = pltpu.make_async_copy(mixed, mixed_ref.at[0], sems.at[5])
    for copy in (gain_copy, frame_copy, *weight_copies):
        copy.start()
    gain_copy.wait()
    frame_copy.wait()
    floats = frame[...].astype(jnp.float32)
    rows = normed(floats, gains[0:1]).astype(jnp.bfloat16)
    for copy in weight_copies:
        copy.wait()
    heads = jnp.dot(rows, project[...], preferred_element_type=jnp.float32).astype(jnp.bfloat16)
    context = attend(heads, None)
    here = (floats + jnp.dot(context, output[...], preferred_element_type=jnp.float32)).astype(jnp.bfloat16)
    mixed[...] = here
    mixed_copy.start()
    sent = normed(here.astype(jnp.float32), gains[1:2])
    put(sent.reshape(scratch.shape).astype(jnp.bfloat16), scratch, sent_refs, groups)
    mixed_copy.wait()


def space_kernel(groups, extra, video_ref, gain_ref, project_ref, output_ref, time_gain_ref, *refs):
    mixed_ref, *sent_refs = refs[extra:]
    sent_refs, scratch = (sent_refs, None) if groups is None else (sent_refs[:-1], sent_refs[-1])
    floats = video_ref[0].astype(jnp.float32)
    heads = jnp.dot(
        normed(floats, gain_ref[...]).astype(jnp.bfloat16), project_ref[...], preferred_element_type=jnp.float32
    ).astype(jnp.bfloat16)
    context = attend(heads, None)
    mixed = (floats + jnp.dot(context, output_ref[...], preferred_element_type=jnp.float32)).astype(jnp.bfloat16)
    mixed_ref[0] = mixed
    sent = normed(mixed.astype(jnp.float32), time_gain_ref[...])
    shape = sent_refs[0].shape if groups is None else scratch.shape
    put(sent.reshape(shape).astype(jnp.bfloat16), scratch, sent_refs, groups)


def time_kernel(groups, back, extra, patch_here, rows_ref, project_ref, *refs):
    *context_refs, bias_ref = refs[extra:]
    context_refs, scratch = (context_refs, None) if back is None else (context_refs[:-1], context_refs[-1])
    rows, width = bias_ref.shape[0], rows_ref.shape[-1]

    @pl.when(pl.program_id(0) == 0)
    def _():
        query = lax.broadcasted_iota(jnp.int32, (rows, rows), 0)
        key = lax.broadcasted_iota(jnp.int32, (rows, rows), 1)
        seen = (key <= query) & (lax.rem(query, patch_here) == lax.rem(key, patch_here))
        bias_ref[...] = jnp.where(seen, 0.0, MASKED)

    arrived = take(rows_ref, groups).astype(jnp.float32).reshape(rows, width).astype(jnp.bfloat16)
    heads = jnp.dot(arrived, project_ref[...], preferred_element_type=jnp.float32).astype(jnp.bfloat16)
    context = attend(heads, bias_ref[...]).astype(jnp.float32)
    shape = context_refs[0].shape if back is None else scratch.shape
    put(context.reshape(shape).astype(jnp.bfloat16), scratch, context_refs, back)


def time_wide_kernel(
    patch_here, rows_ref, project_ref, before_ref, context_ref, bias_ref, project, heads, contexts, weight_sems, out_sems
):
    clips, rows, width = heads.shape[0], bias_ref.shape[0], rows_ref.shape[-1]
    tile = heads.shape[2] // weight_sems.shape[0]

    def columns(piece):
        return pl.ds(piece * tile, tile)

    def leaving(clip):
        return pltpu.make_async_copy(contexts.at[clip], context_ref.at[:, clip], out_sems.at[clip])

    weights = [
        pltpu.make_async_copy(project_ref.at[:, columns(piece)], project.at[:, columns(piece)], weight_sems.at[piece])
        for piece in range(weight_sems.shape[0])
    ]
    for copy in weights:
        copy.start()
    query = lax.broadcasted_iota(jnp.int32, (rows, rows), 0)
    key = lax.broadcasted_iota(jnp.int32, (rows, rows), 1)
    seen = (key <= query) & (lax.rem(query, patch_here) == lax.rem(key, patch_here))
    bias_ref[...] = jnp.where(seen, 0.0, MASKED)
    arrived = [rows_ref[:, clip].astype(jnp.float32).reshape(rows, width).astype(jnp.bfloat16) for clip in range(clips)]
    for piece, copy in enumerate(weights):
        copy.wait()
        for at, one in enumerate(arrived):
            got = jnp.dot(one, project[:, columns(piece)], preferred_element_type=jnp.float32).astype(jnp.bfloat16)
            heads[at, :, columns(piece)] = got
    for clip in range(clips):
        context = attend(heads[clip], bias_ref[...])
        contexts[clip] = context.astype(jnp.float32).reshape(contexts.shape[1:]).astype(jnp.bfloat16)
        leaving(clip).start()
    for clip in range(clips):
        leaving(clip).wait()


def final_kernel(order, mixed_ref, context_ref, output_ref, *refs):
    out_ref = refs[-1]
    rows = mixed_ref.shape[1]
    context = take(context_ref, order).astype(jnp.float32).reshape(rows, WIDTH).astype(jnp.bfloat16)
    update = jnp.dot(context, output_ref[...], preferred_element_type=jnp.float32)
    out_ref[0] = (mixed_ref[0].astype(jnp.float32) + update).astype(jnp.bfloat16)


def final_wide_kernel(first, mixed_ref, context_ref, output_ref, before_ref, out_ref, done, sems):
    clips, rows, _ = mixed_ref.shape
    part = rows // SPLIT
    copies = []
    for clip in range(clips):
        context = context_ref[:, clip].astype(jnp.float32).reshape(rows, WIDTH).astype(jnp.bfloat16)
        for at in range(SPLIT):
            here = slice(at * part, (at + 1) * part)
            update = jnp.dot(context[here], output_ref[...], preferred_element_type=jnp.float32)
            done[clip, here] = (mixed_ref[clip, here].astype(jnp.float32) + update).astype(jnp.bfloat16)
            copies.append(
                pltpu.make_async_copy(
                    done.at[clip, pl.ds(at * part, part)],
                    out_ref.at[first + clip, pl.ds(at * part, part)],
                    sems.at[clip, at],
                )
            )
            copies[-1].start()
    for copy in copies:
        copy.wait()


def whole(shape):
    return pl.BlockSpec(shape, lambda c: (0,) * len(shape))


def exchange_spec(count, patch_here, width):
    if patch_here % 8:
        return pl.BlockSpec((1, count * patch_here, width), lambda c: (c, 0, 0))
    return pl.BlockSpec((count, 1, patch_here, width), lambda c: (0, c, 0, 0))


def exchange_shape(count, clips, patch_here, width):
    if patch_here % 8:
        return jax.ShapeDtypeStruct((clips, count * patch_here, width), jnp.bfloat16)
    return jax.ShapeDtypeStruct((count, clips, patch_here, width), jnp.bfloat16)


def exchange(sent, count, patch_here):
    plain = sent.ndim == 3
    if plain:
        clips, _, width = sent.shape
        sent = sent.reshape(clips, count, patch_here, width).transpose(1, 0, 2, 3)
    arrived = lax.all_to_all(sent, AXES, split_axis=0, concat_axis=0, tiled=True)
    if plain:
        arrived = arrived.transpose(1, 0, 2, 3).reshape(clips, count * patch_here, width)
    return arrived


def in_hbm(array):
    return pltpu.with_memory_space_constraint(array, pltpu.HBM)


def in_vmem(array):
    return pltpu.with_memory_space_constraint(array, pltpu.VMEM)


def load_kernel(array_ref, awaited_ref, loaded_ref, sem):
    copy = pltpu.make_async_copy(array_ref, loaded_ref, sem)
    copy.start()
    copy.wait()


def load(array, awaited):
    return pl.pallas_call(
        load_kernel,
        in_specs=[ANYWHERE, ANYWHERE],
        out_specs=pl.BlockSpec(memory_space=pltpu.VMEM),
        out_shape=pltpu.VMEM(array.shape, array.dtype),
        scratch_shapes=[pltpu.SemaphoreType.DMA],
        cost_estimate=cost(0, 4 * array.size, 0),
        compiler_params=pltpu.CompilerParams(vmem_limit_bytes=2 * 1024 * 1024),
        name="load",
    )(in_hbm(array), awaited)


def after(rows, awaited):
    return pl.pallas_call(
        lambda *refs: None,
        in_specs=[ANYWHERE] * (1 + len(awaited)),
        out_specs=ANYWHERE,
        out_shape=jax.ShapeDtypeStruct(rows.shape, rows.dtype),
        input_output_aliases={0: 0},
        compiler_params=pltpu.CompilerParams(vmem_limit_bytes=2 * 1024 * 1024),
        name="after",
    )(in_hbm(rows), *awaited)


def swap(blocks, groups):
    steps = []
    devices = 1 << len(sum(groups, ()))
    rows = blocks[0].shape[1:]
    blocks = [block.reshape(1, *(1 << len(group) for group in groups[1:]), *rows) for block in blocks]
    for at, group in enumerate(groups):
        arrived = [
            lax.ppermute(block, AXES, [(device, device ^ mask_of(index, group)) for device in range(devices)])
            for index, block in enumerate(blocks)
            if index
        ]
        steps.append(arrived)
        whole_buffer = jnp.concatenate([blocks[0], *arrived], axis=at)
        if at + 1 < len(groups):
            blocks = jnp.split(whole_buffer, 1 << len(groups[at + 1]), axis=at + 1)
    return whole_buffer.reshape(devices, *rows), steps


def cost(macs, bytes_accessed, exps):
    return pl.CostEstimate(flops=2 * macs, bytes_accessed=bytes_accessed, transcendentals=exps)


def sent_specs(count, clips, patch_here, width, order):
    if order is None:
        return [exchange_shape(count, clips, patch_here, width)], [exchange_spec(count, patch_here, width)], []
    parts = 1 << len(order[0])
    shape = exchange_shape(count // parts, clips, patch_here, width)
    spec = exchange_spec(count // parts, patch_here, width)
    return [shape] * parts, [spec] * parts, [pltpu.VMEM((count, patch_here, width), jnp.bfloat16)]


def space_call(video, first, clips, space_gain, space_project, space_output, time_gain, count, before, groups):
    rows, width = video.shape[1:]
    vmem = pl.BlockSpec(memory_space=pltpu.VMEM)
    shapes, specs, scratch = sent_specs(count, clips, rows // count, width, groups)
    mixed, *sent = pl.pallas_call(
        partial(space_kernel, groups, len(before)),
        grid=(clips,),
        in_specs=[
            pl.BlockSpec((1, rows, width), lambda c: (first + c, 0, 0)),
            whole((1, width)),
            whole((width, 3 * WIDTH)),
            whole((WIDTH, width)),
            whole((1, width)),
        ]
        + [ANYWHERE] * len(before),
        out_specs=[pl.BlockSpec((1, rows, width), lambda c: (c, 0, 0)), *specs],
        out_shape=[pltpu.HBM((clips, rows, width), jnp.bfloat16), *(pltpu.HBM(shape.shape, jnp.bfloat16) for shape in shapes)],
        scratch_shapes=scratch,
        cost_estimate=cost(
            clips * rows * (width * 4 * WIDTH + 8 * rows * WIDTH), 2 * (4 * width * WIDTH + 3 * clips * rows * width),
            clips * HEADS * rows * rows,
        ),
        compiler_params=pltpu.CompilerParams(vmem_limit_bytes=SPACE_VMEM_LIMIT),
        name="space",
    )(in_hbm(video), in_hbm(space_gain), in_vmem(space_project), in_vmem(space_output), in_hbm(time_gain), *map(in_hbm, before))
    return mixed, sent


def space_first_call(video, space_gain, space_project, space_output, time_gain, count, groups):
    rows, width = video.shape[1:]
    patch_here = rows // count
    vmem = pl.BlockSpec(memory_space=pltpu.VMEM)
    shapes, _, scratch = sent_specs(count, 1, patch_here, width, groups)
    mixed, project, output, *sent = pl.pallas_call(
        partial(space_first_kernel, groups),
        in_specs=[ANYWHERE] * 5,
        out_specs=[ANYWHERE, vmem, vmem, *[vmem] * len(shapes)],
        out_shape=[
            pltpu.HBM((1, rows, width), jnp.bfloat16),
            pltpu.VMEM(space_project.shape, jnp.bfloat16),
            pltpu.VMEM(space_output.shape, jnp.bfloat16),
            *[pltpu.VMEM(shape.shape, jnp.bfloat16) for shape in shapes],
        ],
        scratch_shapes=[
            pltpu.VMEM((rows, width), jnp.bfloat16),
            pltpu.VMEM((2, width), jnp.float32),
            pltpu.VMEM((rows, width), jnp.bfloat16),
            *scratch,
            pltpu.SemaphoreType.DMA((6,)),
        ],
        cost_estimate=cost(rows * (width * 4 * WIDTH + 8 * rows * WIDTH), 2 * (4 * width * WIDTH + 3 * rows * width), 0),
        compiler_params=pltpu.CompilerParams(vmem_limit_bytes=SPACE_VMEM_LIMIT),
        name="space",
    )(*map(in_hbm, (video, space_gain, space_project, space_output, time_gain)))
    return mixed, project, output, sent


def time_call(arrived, clips, rows, time_project, count, before, groups, back, project=None):
    width = arrived.shape[-1]
    patch_here = rows // count
    shapes, specs, scratch = sent_specs(count, clips, patch_here, WIDTH, back)
    return pl.pallas_call(
        partial(time_kernel, groups, back, len(before), patch_here),
        grid=(clips,),
        in_specs=[exchange_spec(count, patch_here, width), whole((width, 3 * WIDTH)) if project is None else pl.BlockSpec(memory_space=pltpu.VMEM)] + [ANYWHERE] * len(before),
        out_specs=specs,
        out_shape=shapes,
        scratch_shapes=scratch + [pltpu.VMEM((rows, rows), jnp.float32)],
        cost_estimate=cost(
            clips * rows * (width * 3 * WIDTH + 8 * rows * WIDTH), 2 * (3 * width * WIDTH + 2 * clips * rows * width),
            clips * HEADS * rows * rows,
        ),
        compiler_params=pltpu.CompilerParams(vmem_limit_bytes=TIME_VMEM_LIMIT),
        name="time",
    )(arrived, in_hbm(time_project) if project is None else in_vmem(project), *map(in_hbm, before))


def time_wide_call(arrived, clips, rows, time_project, count, before):
    width = arrived.shape[-1]
    patch_here = rows // count
    return pl.pallas_call(
        partial(time_wide_kernel, patch_here),
        in_specs=[pl.BlockSpec(memory_space=pltpu.VMEM), ANYWHERE, ANYWHERE],
        out_specs=ANYWHERE,
        out_shape=pltpu.HBM((count, clips, patch_here, WIDTH), jnp.bfloat16),
        scratch_shapes=[
            pltpu.VMEM((rows, rows), jnp.float32),
            pltpu.VMEM((width, 3 * WIDTH), jnp.bfloat16),
            pltpu.VMEM((clips, rows, 3 * WIDTH), jnp.bfloat16),
            pltpu.VMEM((clips, count, patch_here, WIDTH), jnp.bfloat16),
            pltpu.SemaphoreType.DMA((PIECES,)),
            pltpu.SemaphoreType.DMA((clips,)),
        ],
        cost_estimate=cost(
            clips * rows * (width * 3 * WIDTH + 8 * rows * WIDTH), 2 * (3 * width * WIDTH + 2 * clips * rows * width),
            clips * HEADS * rows * rows,
        ),
        compiler_params=pltpu.CompilerParams(vmem_limit_bytes=TIME_VMEM_LIMIT),
        name="time",
    )(arrived, in_hbm(time_project), in_hbm(before))


def final_call(mixed, context, time_output, count, first, total, before, order):
    clips, rows, width = mixed.shape
    return pl.pallas_call(
        partial(final_kernel, order),
        grid=(clips,),
        in_specs=[
            pl.BlockSpec((1, rows, width), lambda c: (c, 0, 0)),
            exchange_spec(count, rows // count, WIDTH),
            whole((WIDTH, width)),
        ]
        + [ANYWHERE] * len(before),
        out_specs=pl.BlockSpec((1, rows, width), lambda c: (first + c, 0, 0)),
        out_shape=jax.ShapeDtypeStruct((total, rows, width), jnp.bfloat16),
        input_output_aliases={3: 0} if before else {},
        cost_estimate=cost(clips * rows * width * WIDTH, 2 * (width * WIDTH + 3 * clips * rows * width), 0),
        compiler_params=pltpu.CompilerParams(vmem_limit_bytes=FINAL_VMEM_LIMIT),
        name="final",
    )(mixed, context, time_output, *before)


def final_wide_call(mixed, context, time_output, first, total, before):
    clips, rows, width = mixed.shape
    vmem = pl.BlockSpec(memory_space=pltpu.VMEM)
    return pl.pallas_call(
        partial(final_wide_kernel, first),
        in_specs=[vmem, vmem, vmem, ANYWHERE],
        out_specs=ANYWHERE,
        out_shape=jax.ShapeDtypeStruct((total, rows, width), jnp.bfloat16),
        scratch_shapes=[pltpu.VMEM((clips, rows, width), jnp.bfloat16), pltpu.SemaphoreType.DMA((clips, SPLIT))],
        input_output_aliases={3: 0},
        cost_estimate=cost(clips * rows * width * WIDTH, 2 * (width * WIDTH + 3 * clips * rows * width), 0),
        compiler_params=pltpu.CompilerParams(vmem_limit_bytes=FINAL_VMEM_LIMIT),
        name="final",
    )(mixed, context, time_output, before)


def per_device(video_in, space_gain, space_project, space_output, time_gain, time_project, time_output):
    clip_count, frame_local, patch_count, width = video_in.shape
    count = lax.axis_size("grp") * lax.axis_size("dev")
    patch_here = patch_count // count
    video = video_in.reshape(clip_count, patch_count, width)
    weights = space_gain.reshape(1, width), space_project, space_output, time_gain.reshape(1, width)
    swappable = patch_here % 8 == 0 and count & (count - 1) == 0
    if not swappable:
        return plainly(video, weights, time_project, time_output, count).reshape(video_in.shape)
    others = clip_count - 1
    back = bit_groups()
    there = [back[2], back[0], back[1]]
    kept, project, output, sent = space_first_call(video, *weights, count, there)
    weights = weights[0], project, output, weights[3]
    kept_others, sent_others = space_call(video, 1, others, *weights, count, [kept], None)
    arrived, steps = swap(sent, there)
    arrived_others = exchange(after(sent_others[0], steps[0]), count, patch_here)
    loaded = load(time_project, steps[1][0])
    context = time_call(arrived, 1, patch_count, time_project, count, [], there, back, loaded)
    returned, steps = swap(context, back)
    context = time_wide_call(arrived_others, others, patch_count, time_project, count, context[0])
    returned_others = exchange(after(context, steps[-1]), count, patch_here)
    out = final_call(kept, returned, time_output, count, 0, clip_count, [], back)
    out = final_wide_call(kept_others, returned_others, time_output, 1, clip_count, out)
    return out.reshape(clip_count, frame_local, patch_count, width)


def plainly(video, weights, time_project, time_output, count):
    clips, rows, _ = video.shape
    kept, sent = space_call(video, 0, clips, *weights, count, [], None)
    arrived = exchange(sent[0], count, rows // count)
    context = time_call(arrived, clips, rows, time_project, count, [], None, None)
    returned = exchange(context[0], count, rows // count)
    return final_call(kept, returned, time_output, count, 0, clips, [], None)


def solution(mesh):
    in_specs = (P(None, AXES, None, None), P(), P(), P(), P(), P(), P())
    return jax.shard_map(
        per_device, mesh=mesh, in_specs=in_specs, out_specs=P(None, AXES, None, None), check_vma=False
    )
```

```python
from functools import partial

import jax
import jax.numpy as jnp
from jax import lax
from jax.experimental import pallas as pl
from jax.experimental.pallas import tpu as pltpu
from jax.sharding import PartitionSpec as P

HEADS = 8
HEAD_DIM = 64
WIDTH = HEADS * HEAD_DIM
LANES = 128
EPSILON = 1e-06
MASKED = -1e30
SPACE_VMEM_LIMIT = 40 * 1024 * 1024
SPLIT = 2
PIECES = 3
ANYWHERE = pl.BlockSpec(memory_space=pl.ANY)
AXES = ("grp", "dev")
VMEM_LIMIT = 60 * 1024 * 1024
TIME_VMEM_LIMIT = 40 * 1024 * 1024
FINAL_VMEM_LIMIT = 40 * 1024 * 1024


def normed(floats, gain):
    centred = floats - jnp.mean(floats, axis=-1, keepdims=True)
    spread = jnp.mean(jnp.square(centred), axis=-1, keepdims=True)
    return centred * lax.rsqrt(spread + EPSILON) * gain


def attend(heads, bias):
    rows = heads.shape[0]
    low = lax.broadcasted_iota(jnp.int32, (rows, LANES), 1) < HEAD_DIM
    ones = jnp.ones((rows, LANES), jnp.bfloat16)
    contexts, pending = [], []
    for pair in range(WIDTH // LANES):
        at = pair * LANES
        queries = heads[:, at : at + LANES] * jnp.bfloat16(HEAD_DIM**-0.5)
        keys = heads[:, WIDTH + at : WIDTH + at + LANES]
        values = heads[:, 2 * WIDTH + at : 2 * WIDTH + at + LANES]
        nothing = jnp.zeros_like(queries)
        stacked = jnp.concatenate([jnp.where(low, queries, nothing), jnp.where(low, nothing, queries)], axis=0)
        scores = lax.dot_general(stacked, keys, (((1,), (1,)), ((), ())), preferred_element_type=jnp.float32)
        if bias is not None:
            scores = scores + jnp.concatenate([bias, bias], axis=0)
        weights = jnp.exp(scores - jnp.max(scores, axis=-1, keepdims=True)).astype(jnp.bfloat16)
        pending.append((weights, values))
    for weights, values in pending:
        sums = jnp.dot(weights, jnp.concatenate([values, ones], axis=1), preferred_element_type=jnp.float32)
        context = sums[:, :LANES] / sums[:, LANES:]
        contexts.append(jnp.where(low, context[:rows], context[rows:]))
    return jnp.concatenate(contexts, axis=1).astype(jnp.bfloat16)


def bit_groups():
    inner = lax.axis_size("dev").bit_length() - 1
    bits = inner + lax.axis_size("grp").bit_length() - 1
    return [(inner,), (0, *reversed(range(inner + 1, bits))), tuple(reversed(range(1, inner)))]


def mask_of(index, group):
    return sum(((index >> (len(group) - 1 - at)) & 1) << bit for at, bit in enumerate(group))


def put(parts, scratch, out_refs, groups):
    if groups is None:
        out_refs[0][...] = parts.reshape(out_refs[0].shape)
        return
    scratch[...] = parts
    me = lax.axis_index(AXES)
    order = sum(groups, ())
    size = out_refs[0].shape[0]
    for place in range(size * len(out_refs)):
        out_refs[place // size][place % size, 0] = scratch[mask_of(place, order) ^ me]


def take(ref, groups):
    if groups is None:
        return ref[...]
    me = lax.axis_index(AXES)
    order = sum(groups, ())
    parts = []
    for device in range(ref.shape[0]):
        slot = device ^ me
        place = sum(((slot >> bit) & 1) << (len(order) - 1 - at) for at, bit in enumerate(order))
        parts.append(ref[place, 0])
    return jnp.stack(parts)


def space_first_kernel(
    groups, video_ref, gain_ref, project_ref, output_ref, time_gain_ref, mixed_ref, project, output, *refs
):
    *sent_refs, frame, gains, mixed, scratch, sems = refs
    parts = sent_refs[0].shape[0]
    frame_copy = pltpu.make_async_copy(video_ref.at[0], frame, sems.at[0])
    gain_copy = pltpu.make_async_copy(gain_ref, gains.at[pl.ds(0, 1)], sems.at[1])
    weight_copies = [
        pltpu.make_async_copy(project_ref, project, sems.at[2]),
        pltpu.make_async_copy(output_ref, output, sems.at[3]),
        pltpu.make_async_copy(time_gain_ref, gains.at[pl.ds(1, 1)], sems.at[4]),
    ]
    mixed_copy = pltpu.make_async_copy(mixed, mixed_ref.at[0], sems.at[5])
    for copy in (gain_copy, frame_copy, *weight_copies):
        copy.start()
    gain_copy.wait()
    frame_copy.wait()
    floats = frame[...].astype(jnp.float32)
    rows = normed(floats, gains[0:1]).astype(jnp.bfloat16)
    for copy in weight_copies:
        copy.wait()
    heads = jnp.dot(rows, project[...], preferred_element_type=jnp.float32).astype(jnp.bfloat16)
    context = attend(heads, None)
    here = (floats + jnp.dot(context, output[...], preferred_element_type=jnp.float32)).astype(jnp.bfloat16)
    mixed[...] = here
    mixed_copy.start()
    sent = normed(here.astype(jnp.float32), gains[1:2])
    put(sent.reshape(scratch.shape).astype(jnp.bfloat16), scratch, sent_refs, groups)
    mixed_copy.wait()


def space_kernel(groups, extra, video_ref, gain_ref, project_ref, output_ref, time_gain_ref, *refs):
    mixed_ref, *sent_refs = refs[extra:]
    sent_refs, scratch = (sent_refs, None) if groups is None else (sent_refs[:-1], sent_refs[-1])
    floats = video_ref[0].astype(jnp.float32)
    heads = jnp.dot(
        normed(floats, gain_ref[...]).astype(jnp.bfloat16), project_ref[...], preferred_element_type=jnp.float32
    ).astype(jnp.bfloat16)
    context = attend(heads, None)
    mixed = (floats + jnp.dot(context, output_ref[...], preferred_element_type=jnp.float32)).astype(jnp.bfloat16)
    mixed_ref[0] = mixed
    sent = normed(mixed.astype(jnp.float32), time_gain_ref[...])
    shape = sent_refs[0].shape if groups is None else scratch.shape
    put(sent.reshape(shape).astype(jnp.bfloat16), scratch, sent_refs, groups)


def time_kernel(groups, back, extra, patch_here, rows_ref, project_ref, *refs):
    *context_refs, bias_ref = refs[extra:]
    context_refs, scratch = (context_refs, None) if back is None else (context_refs[:-1], context_refs[-1])
    rows, width = bias_ref.shape[0], rows_ref.shape[-1]

    @pl.when(pl.program_id(0) == 0)
    def _():
        query = lax.broadcasted_iota(jnp.int32, (rows, rows), 0)
        key = lax.broadcasted_iota(jnp.int32, (rows, rows), 1)
        seen = (key <= query) & (lax.rem(query, patch_here) == lax.rem(key, patch_here))
        bias_ref[...] = jnp.where(seen, 0.0, MASKED)

    arrived = take(rows_ref, groups).astype(jnp.float32).reshape(rows, width).astype(jnp.bfloat16)
    heads = jnp.dot(arrived, project_ref[...], preferred_element_type=jnp.float32).astype(jnp.bfloat16)
    context = attend(heads, bias_ref[...]).astype(jnp.float32)
    shape = context_refs[0].shape if back is None else scratch.shape
    put(context.reshape(shape).astype(jnp.bfloat16), scratch, context_refs, back)


def time_wide_kernel(
    patch_here, rows_ref, project_ref, before_ref, context_ref, bias_ref, project, heads, contexts, weight_sems, out_sems
):
    clips, rows, width = heads.shape[0], bias_ref.shape[0], rows_ref.shape[-1]
    tile = heads.shape[2] // weight_sems.shape[0]

    def columns(piece):
        return pl.ds(piece * tile, tile)

    def leaving(clip):
        return pltpu.make_async_copy(contexts.at[clip], context_ref.at[:, clip], out_sems.at[clip])

    weights = [
        pltpu.make_async_copy(project_ref.at[:, columns(piece)], project.at[:, columns(piece)], weight_sems.at[piece])
        for piece in range(weight_sems.shape[0])
    ]
    for copy in weights:
        copy.start()
    query = lax.broadcasted_iota(jnp.int32, (rows, rows), 0)
    key = lax.broadcasted_iota(jnp.int32, (rows, rows), 1)
    seen = (key <= query) & (lax.rem(query, patch_here) == lax.rem(key, patch_here))
    bias_ref[...] = jnp.where(seen, 0.0, MASKED)
    arrived = [rows_ref[:, clip].astype(jnp.float32).reshape(rows, width).astype(jnp.bfloat16) for clip in range(clips)]
    for piece, copy in enumerate(weights):
        copy.wait()
        for at, one in enumerate(arrived):
            got = jnp.dot(one, project[:, columns(piece)], preferred_element_type=jnp.float32).astype(jnp.bfloat16)
            heads[at, :, columns(piece)] = got
    for clip in range(clips):
        context = attend(heads[clip], bias_ref[...])
        contexts[clip] = context.astype(jnp.float32).reshape(contexts.shape[1:]).astype(jnp.bfloat16)
        leaving(clip).start()
    for clip in range(clips):
        leaving(clip).wait()


def final_kernel(order, mixed_ref, context_ref, output_ref, *refs):
    out_ref = refs[-1]
    rows = mixed_ref.shape[1]
    context = take(context_ref, order).astype(jnp.float32).reshape(rows, WIDTH).astype(jnp.bfloat16)
    update = jnp.dot(context, output_ref[...], preferred_element_type=jnp.float32)
    out_ref[0] = (mixed_ref[0].astype(jnp.float32) + update).astype(jnp.bfloat16)


def final_wide_kernel(first, mixed_ref, context_ref, output_ref, before_ref, out_ref, done, sems):
    clips, rows, _ = mixed_ref.shape
    part = rows // SPLIT
    copies = []
    for clip in range(clips):
        context = context_ref[:, clip].astype(jnp.float32).reshape(rows, WIDTH).astype(jnp.bfloat16)
        for at in range(SPLIT):
            here = slice(at * part, (at + 1) * part)
            update = jnp.dot(context[here], output_ref[...], preferred_element_type=jnp.float32)
            done[clip, here] = (mixed_ref[clip, here].astype(jnp.float32) + update).astype(jnp.bfloat16)
            copies.append(
                pltpu.make_async_copy(
                    done.at[clip, pl.ds(at * part, part)],
                    out_ref.at[first + clip, pl.ds(at * part, part)],
                    sems.at[clip, at],
                )
            )
            copies[-1].start()
    for copy in copies:
        copy.wait()


def whole(shape):
    return pl.BlockSpec(shape, lambda c: (0,) * len(shape))


def exchange_spec(count, patch_here, width):
    if patch_here % 8:
        return pl.BlockSpec((1, count * patch_here, width), lambda c: (c, 0, 0))
    return pl.BlockSpec((count, 1, patch_here, width), lambda c: (0, c, 0, 0))


def exchange_shape(count, clips, patch_here, width):
    if patch_here % 8:
        return jax.ShapeDtypeStruct((clips, count * patch_here, width), jnp.bfloat16)
    return jax.ShapeDtypeStruct((count, clips, patch_here, width), jnp.bfloat16)


def exchange(sent, count, patch_here):
    plain = sent.ndim == 3
    if plain:
        clips, _, width = sent.shape
        sent = sent.reshape(clips, count, patch_here, width).transpose(1, 0, 2, 3)
    arrived = lax.all_to_all(sent, AXES, split_axis=0, concat_axis=0, tiled=True)
    if plain:
        arrived = arrived.transpose(1, 0, 2, 3).reshape(clips, count * patch_here, width)
    return arrived


def in_hbm(array):
    return pltpu.with_memory_space_constraint(array, pltpu.HBM)


def in_vmem(array):
    return pltpu.with_memory_space_constraint(array, pltpu.VMEM)


def load_kernel(array_ref, awaited_ref, loaded_ref, sem):
    copy = pltpu.make_async_copy(array_ref, loaded_ref, sem)
    copy.start()
    copy.wait()


def load(array, awaited):
    return pl.pallas_call(
        load_kernel,
        in_specs=[ANYWHERE, ANYWHERE],
        out_specs=pl.BlockSpec(memory_space=pltpu.VMEM),
        out_shape=pltpu.VMEM(array.shape, array.dtype),
        scratch_shapes=[pltpu.SemaphoreType.DMA],
        cost_estimate=cost(0, 4 * array.size, 0),
        compiler_params=pltpu.CompilerParams(vmem_limit_bytes=2 * 1024 * 1024),
        name="load",
    )(in_hbm(array), awaited)


def after(rows, awaited):
    return pl.pallas_call(
        lambda *refs: None,
        in_specs=[ANYWHERE] * (1 + len(awaited)),
        out_specs=ANYWHERE,
        out_shape=jax.ShapeDtypeStruct(rows.shape, rows.dtype),
        input_output_aliases={0: 0},
        compiler_params=pltpu.CompilerParams(vmem_limit_bytes=2 * 1024 * 1024),
        name="after",
    )(in_hbm(rows), *awaited)


def swap(blocks, groups):
    steps = []
    devices = 1 << len(sum(groups, ()))
    rows = blocks[0].shape[1:]
    blocks = [block.reshape(1, *(1 << len(group) for group in groups[1:]), *rows) for block in blocks]
    for at, group in enumerate(groups):
        arrived = [
            lax.ppermute(block, AXES, [(device, device ^ mask_of(index, group)) for device in range(devices)])
            for index, block in enumerate(blocks)
            if index
        ]
        steps.append(arrived)
        whole_buffer = jnp.concatenate([blocks[0], *arrived], axis=at)
        if at + 1 < len(groups):
            blocks = jnp.split(whole_buffer, 1 << len(groups[at + 1]), axis=at + 1)
    return whole_buffer.reshape(devices, *rows), steps


def cost(macs, bytes_accessed, exps):
    return pl.CostEstimate(flops=2 * macs, bytes_accessed=bytes_accessed, transcendentals=exps)


def sent_specs(count, clips, patch_here, width, order):
    if order is None:
        return [exchange_shape(count, clips, patch_here, width)], [exchange_spec(count, patch_here, width)], []
    parts = 1 << len(order[0])
    shape = exchange_shape(count // parts, clips, patch_here, width)
    spec = exchange_spec(count // parts, patch_here, width)
    return [shape] * parts, [spec] * parts, [pltpu.VMEM((count, patch_here, width), jnp.bfloat16)]


def space_call(video, first, clips, space_gain, space_project, space_output, time_gain, count, before, groups):
    rows, width = video.shape[1:]
    vmem = pl.BlockSpec(memory_space=pltpu.VMEM)
    shapes, specs, scratch = sent_specs(count, clips, rows // count, width, groups)
    mixed, *sent = pl.pallas_call(
        partial(space_kernel, groups, len(before)),
        grid=(clips,),
        in_specs=[
            pl.BlockSpec((1, rows, width), lambda c: (first + c, 0, 0)),
            whole((1, width)),
            whole((width, 3 * WIDTH)),
            whole((WIDTH, width)),
            whole((1, width)),
        ]
        + [ANYWHERE] * len(before),
        out_specs=[pl.BlockSpec((1, rows, width), lambda c: (c, 0, 0)), *specs],
        out_shape=[pltpu.HBM((clips, rows, width), jnp.bfloat16), *(pltpu.HBM(shape.shape, jnp.bfloat16) for shape in shapes)],
        scratch_shapes=scratch,
        cost_estimate=cost(
            clips * rows * (width * 4 * WIDTH + 8 * rows * WIDTH), 2 * (4 * width * WIDTH + 3 * clips * rows * width),
            clips * HEADS * rows * rows,
        ),
        compiler_params=pltpu.CompilerParams(vmem_limit_bytes=SPACE_VMEM_LIMIT),
        name="space",
    )(in_hbm(video), in_hbm(space_gain), in_vmem(space_project), in_vmem(space_output), in_hbm(time_gain), *map(in_hbm, before))
    return mixed, sent


def space_first_call(video, space_gain, space_project, space_output, time_gain, count, groups):
    rows, width = video.shape[1:]
    patch_here = rows // count
    vmem = pl.BlockSpec(memory_space=pltpu.VMEM)
    shapes, _, scratch = sent_specs(count, 1, patch_here, width, groups)
    mixed, project, output, *sent = pl.pallas_call(
        partial(space_first_kernel, groups),
        in_specs=[ANYWHERE] * 5,
        out_specs=[ANYWHERE, vmem, vmem, *[vmem] * len(shapes)],
        out_shape=[
            pltpu.HBM((1, rows, width), jnp.bfloat16),
            pltpu.VMEM(space_project.shape, jnp.bfloat16),
            pltpu.VMEM(space_output.shape, jnp.bfloat16),
            *[pltpu.VMEM(shape.shape, jnp.bfloat16) for shape in shapes],
        ],
        scratch_shapes=[
            pltpu.VMEM((rows, width), jnp.bfloat16),
            pltpu.VMEM((2, width), jnp.float32),
            pltpu.VMEM((rows, width), jnp.bfloat16),
            *scratch,
            pltpu.SemaphoreType.DMA((6,)),
        ],
        cost_estimate=cost(rows * (width * 4 * WIDTH + 8 * rows * WIDTH), 2 * (4 * width * WIDTH + 3 * rows * width), 0),
        compiler_params=pltpu.CompilerParams(vmem_limit_bytes=SPACE_VMEM_LIMIT),
        name="space",
    )(*map(in_hbm, (video, space_gain, space_project, space_output, time_gain)))
    return mixed, project, output, sent


def time_call(arrived, clips, rows, time_project, count, before, groups, back, project=None):
    width = arrived.shape[-1]
    patch_here = rows // count
    shapes, specs, scratch = sent_specs(count, clips, patch_here, WIDTH, back)
    return pl.pallas_call(
        partial(time_kernel, groups, back, len(before), patch_here),
        grid=(clips,),
        in_specs=[exchange_spec(count, patch_here, width), whole((width, 3 * WIDTH)) if project is None else pl.BlockSpec(memory_space=pltpu.VMEM)] + [ANYWHERE] * len(before),
        out_specs=specs,
        out_shape=shapes,
        scratch_shapes=scratch + [pltpu.VMEM((rows, rows), jnp.float32)],
        cost_estimate=cost(
            clips * rows * (width * 3 * WIDTH + 8 * rows * WIDTH), 2 * (3 * width * WIDTH + 2 * clips * rows * width),
            clips * HEADS * rows * rows,
        ),
        compiler_params=pltpu.CompilerParams(vmem_limit_bytes=TIME_VMEM_LIMIT),
        name="time",
    )(arrived, in_hbm(time_project) if project is None else in_vmem(project), *map(in_hbm, before))


def time_wide_call(arrived, clips, rows, time_project, count, before):
    width = arrived.shape[-1]
    patch_here = rows // count
    return pl.pallas_call(
        partial(time_wide_kernel, patch_here),
        in_specs=[pl.BlockSpec(memory_space=pltpu.VMEM), ANYWHERE, ANYWHERE],
        out_specs=ANYWHERE,
        out_shape=pltpu.HBM((count, clips, patch_here, WIDTH), jnp.bfloat16),
        scratch_shapes=[
            pltpu.VMEM((rows, rows), jnp.float32),
            pltpu.VMEM((width, 3 * WIDTH), jnp.bfloat16),
            pltpu.VMEM((clips, rows, 3 * WIDTH), jnp.bfloat16),
            pltpu.VMEM((clips, count, patch_here, WIDTH), jnp.bfloat16),
            pltpu.SemaphoreType.DMA((PIECES,)),
            pltpu.SemaphoreType.DMA((clips,)),
        ],
        cost_estimate=cost(
            clips * rows * (width * 3 * WIDTH + 8 * rows * WIDTH), 2 * (3 * width * WIDTH + 2 * clips * rows * width),
            clips * HEADS * rows * rows,
        ),
        compiler_params=pltpu.CompilerParams(vmem_limit_bytes=TIME_VMEM_LIMIT),
        name="time",
    )(arrived, in_hbm(time_project), in_hbm(before))


def final_call(mixed, context, time_output, count, first, total, before, order):
    clips, rows, width = mixed.shape
    return pl.pallas_call(
        partial(final_kernel, order),
        grid=(clips,),
        in_specs=[
            pl.BlockSpec((1, rows, width), lambda c: (c, 0, 0)),
            exchange_spec(count, rows // count, WIDTH),
            whole((WIDTH, width)),
        ]
        + [ANYWHERE] * len(before),
        out_specs=pl.BlockSpec((1, rows, width), lambda c: (first + c, 0, 0)),
        out_shape=jax.ShapeDtypeStruct((total, rows, width), jnp.bfloat16),
        input_output_aliases={3: 0} if before else {},
        cost_estimate=cost(clips * rows * width * WIDTH, 2 * (width * WIDTH + 3 * clips * rows * width), 0),
        compiler_params=pltpu.CompilerParams(vmem_limit_bytes=FINAL_VMEM_LIMIT),
        name="final",
    )(mixed, context, time_output, *before)


def final_wide_call(mixed, context, time_output, first, total, before):
    clips, rows, width = mixed.shape
    vmem = pl.BlockSpec(memory_space=pltpu.VMEM)
    return pl.pallas_call(
        partial(final_wide_kernel, first),
        in_specs=[vmem, vmem, vmem, ANYWHERE],
        out_specs=ANYWHERE,
        out_shape=jax.ShapeDtypeStruct((total, rows, width), jnp.bfloat16),
        scratch_shapes=[pltpu.VMEM((clips, rows, width), jnp.bfloat16), pltpu.SemaphoreType.DMA((clips, SPLIT))],
        input_output_aliases={3: 0},
        cost_estimate=cost(clips * rows * width * WIDTH, 2 * (width * WIDTH + 3 * clips * rows * width), 0),
        compiler_params=pltpu.CompilerParams(vmem_limit_bytes=FINAL_VMEM_LIMIT),
        name="final",
    )(mixed, context, time_output, before)


def per_device(video_in, space_gain, space_project, space_output, time_gain, time_project, time_output):
    clip_count, frame_local, patch_count, width = video_in.shape
    count = lax.axis_size("grp") * lax.axis_size("dev")
    patch_here = patch_count // count
    video = video_in.reshape(clip_count, patch_count, width)
    weights = space_gain.reshape(1, width), space_project, space_output, time_gain.reshape(1, width)
    swappable = patch_here % 8 == 0 and count & (count - 1) == 0
    if not swappable:
        return plainly(video, weights, time_project, time_output, count).reshape(video_in.shape)
    others = clip_count - 1
    core, near, far = bit_groups()
    there, back = [far, core, near], [near, far, core]
    kept, project, output, sent = space_first_call(video, *weights, count, there)
    weights = weights[0], project, output, weights[3]
    kept_others, sent_others = space_call(video, 1, others, *weights, count, [kept], None)
    arrived, steps = swap(sent, there)
    arrived_others = exchange(after(sent_others[0], steps[0]), count, patch_here)
    loaded = load(time_project, steps[1][0])
    context = time_call(arrived, 1, patch_count, time_project, count, [], there, back, loaded)
    returned, steps = swap(context, back)
    context = time_wide_call(arrived_others, others, patch_count, time_project, count, context[0])
    returned_others = exchange(after(context, steps[1]), count, patch_here)
    out = final_call(kept, returned, time_output, count, 0, clip_count, [], back)
    out = final_wide_call(kept_others, returned_others, time_output, 1, clip_count, out)
    return out.reshape(clip_count, frame_local, patch_count, width)


def plainly(video, weights, time_project, time_output, count):
    clips, rows, _ = video.shape
    kept, sent = space_call(video, 0, clips, *weights, count, [], None)
    arrived = exchange(sent[0], count, rows // count)
    context = time_call(arrived, clips, rows, time_project, count, [], None, None)
    returned = exchange(context[0], count, rows // count)
    return final_call(kept, returned, time_output, count, 0, clips, [], None)


def solution(mesh):
    in_specs = (P(None, AXES, None, None), P(), P(), P(), P(), P(), P())
    return jax.shard_map(
        per_device, mesh=mesh, in_specs=in_specs, out_specs=P(None, AXES, None, None), check_vma=False
    )
```

```python
from functools import partial

import jax
import jax.numpy as jnp
from jax import lax
from jax.experimental import pallas as pl
from jax.experimental.pallas import tpu as pltpu
from jax.sharding import PartitionSpec as P

HEADS = 8
HEAD_DIM = 64
WIDTH = HEADS * HEAD_DIM
LANES = 128
EPSILON = 1e-06
MASKED = -1e30
SPACE_VMEM_LIMIT = 40 * 1024 * 1024
SPLIT = 2
PIECES = 3
ANYWHERE = pl.BlockSpec(memory_space=pl.ANY)
AXES = ("grp", "dev")
VMEM_LIMIT = 60 * 1024 * 1024
TIME_VMEM_LIMIT = 40 * 1024 * 1024
FINAL_VMEM_LIMIT = 40 * 1024 * 1024


def normed(floats, gain):
    centred = floats - jnp.mean(floats, axis=-1, keepdims=True)
    spread = jnp.mean(jnp.square(centred), axis=-1, keepdims=True)
    return centred * lax.rsqrt(spread + EPSILON) * gain


def attend(heads, bias):
    rows = heads.shape[0]
    low = lax.broadcasted_iota(jnp.int32, (rows, LANES), 1) < HEAD_DIM
    ones = jnp.ones((rows, LANES), jnp.bfloat16)
    contexts, pending = [], []
    for pair in range(WIDTH // LANES):
        at = pair * LANES
        queries = heads[:, at : at + LANES] * jnp.bfloat16(HEAD_DIM**-0.5)
        keys = heads[:, WIDTH + at : WIDTH + at + LANES]
        values = heads[:, 2 * WIDTH + at : 2 * WIDTH + at + LANES]
        nothing = jnp.zeros_like(queries)
        stacked = jnp.concatenate([jnp.where(low, queries, nothing), jnp.where(low, nothing, queries)], axis=0)
        scores = lax.dot_general(stacked, keys, (((1,), (1,)), ((), ())), preferred_element_type=jnp.float32)
        if bias is not None:
            scores = scores + jnp.concatenate([bias, bias], axis=0)
        weights = jnp.exp(scores - jnp.max(scores, axis=-1, keepdims=True)).astype(jnp.bfloat16)
        pending.append((weights, values))
    for weights, values in pending:
        sums = jnp.dot(weights, jnp.concatenate([values, ones], axis=1), preferred_element_type=jnp.float32)
        context = sums[:, :LANES] / sums[:, LANES:]
        contexts.append(jnp.where(low, context[:rows], context[rows:]))
    return jnp.concatenate(contexts, axis=1).astype(jnp.bfloat16)


def bit_groups():
    inner = lax.axis_size("dev").bit_length() - 1
    bits = inner + lax.axis_size("grp").bit_length() - 1
    return [(inner,), (0, *reversed(range(inner + 1, bits))), tuple(reversed(range(1, inner)))]


def mask_of(index, group):
    return sum(((index >> (len(group) - 1 - at)) & 1) << bit for at, bit in enumerate(group))


def put(parts, scratch, out_refs, groups):
    if groups is None:
        out_refs[0][...] = parts.reshape(out_refs[0].shape)
        return
    scratch[...] = parts
    me = lax.axis_index(AXES)
    order = sum(groups, ())
    size = out_refs[0].shape[0]
    for place in range(size * len(out_refs)):
        out_refs[place // size][place % size, 0] = scratch[mask_of(place, order) ^ me]


def take(ref, groups):
    if groups is None:
        return ref[...]
    me = lax.axis_index(AXES)
    order = sum(groups, ())
    parts = []
    for device in range(ref.shape[0]):
        slot = device ^ me
        place = sum(((slot >> bit) & 1) << (len(order) - 1 - at) for at, bit in enumerate(order))
        parts.append(ref[place, 0])
    return jnp.stack(parts)


def space_first_kernel(
    groups, video_ref, gain_ref, project_ref, output_ref, time_gain_ref, mixed_ref, project, output, *refs
):
    *sent_refs, frame, gains, scratch, sems = refs
    parts = sent_refs[0].shape[0]
    frame_copy = pltpu.make_async_copy(video_ref.at[0], frame, sems.at[0])
    gain_copy = pltpu.make_async_copy(gain_ref, gains.at[pl.ds(0, 1)], sems.at[1])
    weight_copies = [
        pltpu.make_async_copy(project_ref, project, sems.at[2]),
        pltpu.make_async_copy(output_ref, output, sems.at[3]),
        pltpu.make_async_copy(time_gain_ref, gains.at[pl.ds(1, 1)], sems.at[4]),
    ]
    for copy in (gain_copy, frame_copy, weight_copies[0]):
        copy.start()
    gain_copy.wait()
    frame_copy.wait()
    for copy in weight_copies[1:]:
        copy.start()
    floats = frame[...].astype(jnp.float32)
    rows = normed(floats, gains[0:1]).astype(jnp.bfloat16)
    weight_copies[0].wait()
    heads = jnp.dot(rows, project[...], preferred_element_type=jnp.float32).astype(jnp.bfloat16)
    context = attend(heads, None)
    for copy in weight_copies[1:]:
        copy.wait()
    here = (floats + jnp.dot(context, output[...], preferred_element_type=jnp.float32)).astype(jnp.bfloat16)
    mixed_ref[0] = here
    sent = normed(here.astype(jnp.float32), gains[1:2])
    put(sent.reshape(scratch.shape).astype(jnp.bfloat16), scratch, sent_refs, groups)


def space_kernel(groups, extra, video_ref, gain_ref, project_ref, output_ref, time_gain_ref, *refs):
    if extra:
        before_ref, stored_ref, *refs = refs

        @pl.when(pl.program_id(0) == 0)
        def _():
            stored_ref[...] = before_ref[...]

    mixed_ref, *sent_refs = refs
    sent_refs, scratch = (sent_refs, None) if groups is None else (sent_refs[:-1], sent_refs[-1])
    floats = video_ref[0].astype(jnp.float32)
    heads = jnp.dot(
        normed(floats, gain_ref[...]).astype(jnp.bfloat16), project_ref[...], preferred_element_type=jnp.float32
    ).astype(jnp.bfloat16)
    context = attend(heads, None)
    mixed = (floats + jnp.dot(context, output_ref[...], preferred_element_type=jnp.float32)).astype(jnp.bfloat16)
    mixed_ref[0] = mixed
    sent = normed(mixed.astype(jnp.float32), time_gain_ref[...])
    shape = sent_refs[0].shape if groups is None else scratch.shape
    put(sent.reshape(shape).astype(jnp.bfloat16), scratch, sent_refs, groups)


def time_kernel(groups, back, extra, patch_here, rows_ref, project_ref, *refs):
    *context_refs, bias_ref = refs[extra:]
    context_refs, scratch = (context_refs, None) if back is None else (context_refs[:-1], context_refs[-1])
    rows, width = bias_ref.shape[0], rows_ref.shape[-1]

    @pl.when(pl.program_id(0) == 0)
    def _():
        query = lax.broadcasted_iota(jnp.int32, (rows, rows), 0)
        key = lax.broadcasted_iota(jnp.int32, (rows, rows), 1)
        seen = (key <= query) & (lax.rem(query, patch_here) == lax.rem(key, patch_here))
        bias_ref[...] = jnp.where(seen, 0.0, MASKED)

    arrived = take(rows_ref, groups).astype(jnp.float32).reshape(rows, width).astype(jnp.bfloat16)
    heads = jnp.dot(arrived, project_ref[...], preferred_element_type=jnp.float32).astype(jnp.bfloat16)
    context = attend(heads, bias_ref[...]).astype(jnp.float32)
    shape = context_refs[0].shape if back is None else scratch.shape
    put(context.reshape(shape).astype(jnp.bfloat16), scratch, context_refs, back)


def time_wide_kernel(
    patch_here, rows_ref, project_ref, before_ref, context_ref, bias_ref, project, heads, contexts, weight_sems, out_sems
):
    clips, rows, width = heads.shape[0], bias_ref.shape[0], rows_ref.shape[-1]
    tile = heads.shape[2] // weight_sems.shape[0]

    def columns(piece):
        return pl.ds(piece * tile, tile)

    def leaving(clip):
        return pltpu.make_async_copy(contexts.at[clip], context_ref.at[:, clip], out_sems.at[clip])

    weights = [
        pltpu.make_async_copy(project_ref.at[:, columns(piece)], project.at[:, columns(piece)], weight_sems.at[piece])
        for piece in range(weight_sems.shape[0])
    ]
    for copy in weights:
        copy.start()
    query = lax.broadcasted_iota(jnp.int32, (rows, rows), 0)
    key = lax.broadcasted_iota(jnp.int32, (rows, rows), 1)
    seen = (key <= query) & (lax.rem(query, patch_here) == lax.rem(key, patch_here))
    bias_ref[...] = jnp.where(seen, 0.0, MASKED)
    arrived = [rows_ref[:, clip].astype(jnp.float32).reshape(rows, width).astype(jnp.bfloat16) for clip in range(clips)]
    for piece, copy in enumerate(weights):
        copy.wait()
        for at, one in enumerate(arrived):
            got = jnp.dot(one, project[:, columns(piece)], preferred_element_type=jnp.float32).astype(jnp.bfloat16)
            heads[at, :, columns(piece)] = got
    for clip in range(clips):
        context = attend(heads[clip], bias_ref[...])
        contexts[clip] = context.astype(jnp.float32).reshape(contexts.shape[1:]).astype(jnp.bfloat16)
        leaving(clip).start()
    for clip in range(clips):
        leaving(clip).wait()


def final_kernel(order, mixed_ref, context_ref, output_ref, *refs):
    out_ref = refs[-1]
    rows = mixed_ref.shape[1]
    context = take(context_ref, order).astype(jnp.float32).reshape(rows, WIDTH).astype(jnp.bfloat16)
    update = jnp.dot(context, output_ref[...], preferred_element_type=jnp.float32)
    out_ref[0] = (mixed_ref[0].astype(jnp.float32) + update).astype(jnp.bfloat16)


def final_wide_kernel(first, mixed_ref, context_ref, output_ref, before_ref, out_ref, done, sems):
    clips, rows, _ = mixed_ref.shape
    part = rows // SPLIT
    copies = []
    for clip in range(clips):
        context = context_ref[:, clip].astype(jnp.float32).reshape(rows, WIDTH).astype(jnp.bfloat16)
        for at in range(SPLIT):
            here = slice(at * part, (at + 1) * part)
            update = jnp.dot(context[here], output_ref[...], preferred_element_type=jnp.float32)
            done[clip, here] = (mixed_ref[clip, here].astype(jnp.float32) + update).astype(jnp.bfloat16)
            copies.append(
                pltpu.make_async_copy(
                    done.at[clip, pl.ds(at * part, part)],
                    out_ref.at[first + clip, pl.ds(at * part, part)],
                    sems.at[clip, at],
                )
            )
            copies[-1].start()
    for copy in copies:
        copy.wait()


def whole(shape):
    return pl.BlockSpec(shape, lambda c: (0,) * len(shape))


def exchange_spec(count, patch_here, width):
    if patch_here % 8:
        return pl.BlockSpec((1, count * patch_here, width), lambda c: (c, 0, 0))
    return pl.BlockSpec((count, 1, patch_here, width), lambda c: (0, c, 0, 0))


def exchange_shape(count, clips, patch_here, width):
    if patch_here % 8:
        return jax.ShapeDtypeStruct((clips, count * patch_here, width), jnp.bfloat16)
    return jax.ShapeDtypeStruct((count, clips, patch_here, width), jnp.bfloat16)


def exchange(sent, count, patch_here):
    plain = sent.ndim == 3
    if plain:
        clips, _, width = sent.shape
        sent = sent.reshape(clips, count, patch_here, width).transpose(1, 0, 2, 3)
    arrived = lax.all_to_all(sent, AXES, split_axis=0, concat_axis=0, tiled=True)
    if plain:
        arrived = arrived.transpose(1, 0, 2, 3).reshape(clips, count * patch_here, width)
    return arrived


def in_hbm(array):
    return pltpu.with_memory_space_constraint(array, pltpu.HBM)


def in_vmem(array):
    return pltpu.with_memory_space_constraint(array, pltpu.VMEM)


def load_kernel(array_ref, awaited_ref, loaded_ref, sem):
    copy = pltpu.make_async_copy(array_ref, loaded_ref, sem)
    copy.start()
    copy.wait()


def load(array, awaited):
    return pl.pallas_call(
        load_kernel,
        in_specs=[ANYWHERE, ANYWHERE],
        out_specs=pl.BlockSpec(memory_space=pltpu.VMEM),
        out_shape=pltpu.VMEM(array.shape, array.dtype),
        scratch_shapes=[pltpu.SemaphoreType.DMA],
        cost_estimate=cost(0, 4 * array.size, 0),
        compiler_params=pltpu.CompilerParams(vmem_limit_bytes=2 * 1024 * 1024),
        name="load",
    )(in_hbm(array), awaited)


def after(rows, awaited):
    return pl.pallas_call(
        lambda *refs: None,
        in_specs=[ANYWHERE] * (1 + len(awaited)),
        out_specs=ANYWHERE,
        out_shape=jax.ShapeDtypeStruct(rows.shape, rows.dtype),
        input_output_aliases={0: 0},
        compiler_params=pltpu.CompilerParams(vmem_limit_bytes=2 * 1024 * 1024),
        name="after",
    )(in_hbm(rows), *awaited)


def swap(blocks, groups):
    steps = []
    devices = 1 << len(sum(groups, ()))
    rows = blocks[0].shape[1:]
    blocks = [block.reshape(1, *(1 << len(group) for group in groups[1:]), *rows) for block in blocks]
    for at, group in enumerate(groups):
        arrived = [
            lax.ppermute(block, AXES, [(device, device ^ mask_of(index, group)) for device in range(devices)])
            for index, block in enumerate(blocks)
            if index
        ]
        steps.append(arrived)
        whole_buffer = jnp.concatenate([blocks[0], *arrived], axis=at)
        if at + 1 < len(groups):
            blocks = jnp.split(whole_buffer, 1 << len(groups[at + 1]), axis=at + 1)
    return whole_buffer.reshape(devices, *rows), steps


def cost(macs, bytes_accessed, exps):
    return pl.CostEstimate(flops=2 * macs, bytes_accessed=bytes_accessed, transcendentals=exps)


def sent_specs(count, clips, patch_here, width, order):
    if order is None:
        return [exchange_shape(count, clips, patch_here, width)], [exchange_spec(count, patch_here, width)], []
    parts = 1 << len(order[0])
    shape = exchange_shape(count // parts, clips, patch_here, width)
    spec = exchange_spec(count // parts, patch_here, width)
    return [shape] * parts, [spec] * parts, [pltpu.VMEM((count, patch_here, width), jnp.bfloat16)]


def space_call(video, first, clips, space_gain, space_project, space_output, time_gain, count, before, groups):
    rows, width = video.shape[1:]
    vmem = pl.BlockSpec(memory_space=pltpu.VMEM)
    shapes, specs, scratch = sent_specs(count, clips, rows // count, width, groups)
    outputs = pl.pallas_call(
        partial(space_kernel, groups, len(before)),
        grid=(clips,),
        in_specs=[
            pl.BlockSpec((1, rows, width), lambda c: (first + c, 0, 0)),
            whole((1, width)),
            whole((width, 3 * WIDTH)),
            whole((WIDTH, width)),
            whole((1, width)),
        ]
        + [vmem] * len(before),
        out_specs=[whole((1, rows, width))] * len(before)
        + [pl.BlockSpec((1, rows, width), lambda c: (c, 0, 0)), *specs],
        out_shape=[pltpu.HBM((1, rows, width), jnp.bfloat16)] * len(before)
        + [pltpu.HBM((clips, rows, width), jnp.bfloat16), *(pltpu.HBM(shape.shape, jnp.bfloat16) for shape in shapes)],
        scratch_shapes=scratch,
        cost_estimate=cost(
            clips * rows * (width * 4 * WIDTH + 8 * rows * WIDTH), 2 * (4 * width * WIDTH + 3 * clips * rows * width),
            clips * HEADS * rows * rows,
        ),
        compiler_params=pltpu.CompilerParams(vmem_limit_bytes=SPACE_VMEM_LIMIT),
        name="space",
    )(in_hbm(video), in_hbm(space_gain), in_vmem(space_project), in_vmem(space_output), in_hbm(time_gain), *map(in_vmem, before))
    return outputs[: len(before)], outputs[len(before)], outputs[len(before) + 1 :]


def space_first_call(video, space_gain, space_project, space_output, time_gain, count, groups):
    rows, width = video.shape[1:]
    patch_here = rows // count
    vmem = pl.BlockSpec(memory_space=pltpu.VMEM)
    shapes, _, scratch = sent_specs(count, 1, patch_here, width, groups)
    mixed, project, output, *sent = pl.pallas_call(
        partial(space_first_kernel, groups),
        in_specs=[ANYWHERE] * 5,
        out_specs=[vmem, vmem, vmem, *[vmem] * len(shapes)],
        out_shape=[
            pltpu.VMEM((1, rows, width), jnp.bfloat16),
            pltpu.VMEM(space_project.shape, jnp.bfloat16),
            pltpu.VMEM(space_output.shape, jnp.bfloat16),
            *[pltpu.VMEM(shape.shape, jnp.bfloat16) for shape in shapes],
        ],
        scratch_shapes=[
            pltpu.VMEM((rows, width), jnp.bfloat16),
            pltpu.VMEM((2, width), jnp.float32),
            *scratch,
            pltpu.SemaphoreType.DMA((5,)),
        ],
        cost_estimate=cost(rows * (width * 4 * WIDTH + 8 * rows * WIDTH), 2 * (4 * width * WIDTH + 3 * rows * width), 0),
        compiler_params=pltpu.CompilerParams(vmem_limit_bytes=SPACE_VMEM_LIMIT),
        name="space",
    )(*map(in_hbm, (video, space_gain, space_project, space_output, time_gain)))
    return mixed, project, output, sent


def time_call(arrived, clips, rows, time_project, count, before, groups, back, project=None):
    width = arrived.shape[-1]
    patch_here = rows // count
    shapes, specs, scratch = sent_specs(count, clips, patch_here, WIDTH, back)
    return pl.pallas_call(
        partial(time_kernel, groups, back, len(before), patch_here),
        grid=(clips,),
        in_specs=[exchange_spec(count, patch_here, width), whole((width, 3 * WIDTH)) if project is None else pl.BlockSpec(memory_space=pltpu.VMEM)] + [ANYWHERE] * len(before),
        out_specs=specs,
        out_shape=shapes,
        scratch_shapes=scratch + [pltpu.VMEM((rows, rows), jnp.float32)],
        cost_estimate=cost(
            clips * rows * (width * 3 * WIDTH + 8 * rows * WIDTH), 2 * (3 * width * WIDTH + 2 * clips * rows * width),
            clips * HEADS * rows * rows,
        ),
        compiler_params=pltpu.CompilerParams(vmem_limit_bytes=TIME_VMEM_LIMIT),
        name="time",
    )(arrived, in_hbm(time_project) if project is None else in_vmem(project), *map(in_hbm, before))


def time_wide_call(arrived, clips, rows, time_project, count, before):
    width = arrived.shape[-1]
    patch_here = rows // count
    return pl.pallas_call(
        partial(time_wide_kernel, patch_here),
        in_specs=[pl.BlockSpec(memory_space=pltpu.VMEM), ANYWHERE, ANYWHERE],
        out_specs=ANYWHERE,
        out_shape=pltpu.HBM((count, clips, patch_here, WIDTH), jnp.bfloat16),
        scratch_shapes=[
            pltpu.VMEM((rows, rows), jnp.float32),
            pltpu.VMEM((width, 3 * WIDTH), jnp.bfloat16),
            pltpu.VMEM((clips, rows, 3 * WIDTH), jnp.bfloat16),
            pltpu.VMEM((clips, count, patch_here, WIDTH), jnp.bfloat16),
            pltpu.SemaphoreType.DMA((PIECES,)),
            pltpu.SemaphoreType.DMA((clips,)),
        ],
        cost_estimate=cost(
            clips * rows * (width * 3 * WIDTH + 8 * rows * WIDTH), 2 * (3 * width * WIDTH + 2 * clips * rows * width),
            clips * HEADS * rows * rows,
        ),
        compiler_params=pltpu.CompilerParams(vmem_limit_bytes=TIME_VMEM_LIMIT),
        name="time",
    )(arrived, in_hbm(time_project), in_hbm(before))


def final_call(mixed, context, time_output, count, first, total, before, order):
    clips, rows, width = mixed.shape
    return pl.pallas_call(
        partial(final_kernel, order),
        grid=(clips,),
        in_specs=[
            pl.BlockSpec((1, rows, width), lambda c: (c, 0, 0)),
            exchange_spec(count, rows // count, WIDTH),
            whole((WIDTH, width)),
        ]
        + [ANYWHERE] * len(before),
        out_specs=pl.BlockSpec((1, rows, width), lambda c: (first + c, 0, 0)),
        out_shape=jax.ShapeDtypeStruct((total, rows, width), jnp.bfloat16),
        input_output_aliases={3: 0} if before else {},
        cost_estimate=cost(clips * rows * width * WIDTH, 2 * (width * WIDTH + 3 * clips * rows * width), 0),
        compiler_params=pltpu.CompilerParams(vmem_limit_bytes=FINAL_VMEM_LIMIT),
        name="final",
    )(mixed, context, time_output, *before)


def final_wide_call(mixed, context, time_output, first, total, before):
    clips, rows, width = mixed.shape
    vmem = pl.BlockSpec(memory_space=pltpu.VMEM)
    return pl.pallas_call(
        partial(final_wide_kernel, first),
        in_specs=[vmem, vmem, vmem, ANYWHERE],
        out_specs=ANYWHERE,
        out_shape=jax.ShapeDtypeStruct((total, rows, width), jnp.bfloat16),
        scratch_shapes=[pltpu.VMEM((clips, rows, width), jnp.bfloat16), pltpu.SemaphoreType.DMA((clips, SPLIT))],
        input_output_aliases={3: 0},
        cost_estimate=cost(clips * rows * width * WIDTH, 2 * (width * WIDTH + 3 * clips * rows * width), 0),
        compiler_params=pltpu.CompilerParams(vmem_limit_bytes=FINAL_VMEM_LIMIT),
        name="final",
    )(mixed, context, time_output, before)


def per_device(video_in, space_gain, space_project, space_output, time_gain, time_project, time_output):
    clip_count, frame_local, patch_count, width = video_in.shape
    count = lax.axis_size("grp") * lax.axis_size("dev")
    patch_here = patch_count // count
    video = video_in.reshape(clip_count, patch_count, width)
    weights = space_gain.reshape(1, width), space_project, space_output, time_gain.reshape(1, width)
    swappable = patch_here % 8 == 0 and count & (count - 1) == 0
    if not swappable:
        return plainly(video, weights, time_project, time_output, count).reshape(video_in.shape)
    others = clip_count - 1
    core, near, far = bit_groups()
    there, back = [far, core, near], [near, far, core]
    kept, project, output, sent = space_first_call(video, *weights, count, there)
    weights = weights[0], project, output, weights[3]
    (kept,), kept_others, sent_others = space_call(video, 1, others, *weights, count, [kept], None)
    arrived, steps = swap(sent, there)
    arrived_others = exchange(after(sent_others[0], steps[0]), count, patch_here)
    loaded = load(time_project, steps[1][0])
    context = time_call(arrived, 1, patch_count, time_project, count, [], there, back, loaded)
    returned, steps = swap(context, back)
    context = time_wide_call(arrived_others, others, patch_count, time_project, count, context[0])
    returned_others = exchange(after(context, steps[1]), count, patch_here)
    out = final_call(kept, returned, time_output, count, 0, clip_count, [], back)
    out = final_wide_call(kept_others, returned_others, time_output, 1, clip_count, out)
    return out.reshape(clip_count, frame_local, patch_count, width)


def plainly(video, weights, time_project, time_output, count):
    clips, rows, _ = video.shape
    _, kept, sent = space_call(video, 0, clips, *weights, count, [], None)
    arrived = exchange(sent[0], count, rows // count)
    context = time_call(arrived, clips, rows, time_project, count, [], None, None)
    returned = exchange(context[0], count, rows // count)
    return final_call(kept, returned, time_output, count, 0, clips, [], None)


def solution(mesh):
    in_specs = (P(None, AXES, None, None), P(), P(), P(), P(), P(), P())
    return jax.shard_map(
        per_device, mesh=mesh, in_specs=in_specs, out_specs=P(None, AXES, None, None), check_vma=False
    )
```

```python
from functools import partial

import jax
import jax.numpy as jnp
from jax import lax
from jax.experimental import pallas as pl
from jax.experimental.pallas import tpu as pltpu
from jax.sharding import PartitionSpec as P

HEADS = 8
HEAD_DIM = 64
WIDTH = HEADS * HEAD_DIM
LANES = 128
EPSILON = 1e-06
MASKED = -1e30
SPACE_VMEM_LIMIT = 40 * 1024 * 1024
SPLIT = 2
PIECES = 3
ANYWHERE = pl.BlockSpec(memory_space=pl.ANY)
AXES = ("grp", "dev")
VMEM_LIMIT = 60 * 1024 * 1024
TIME_VMEM_LIMIT = 40 * 1024 * 1024
FINAL_VMEM_LIMIT = 40 * 1024 * 1024


def normed(floats, gain):
    centred = floats - jnp.mean(floats, axis=-1, keepdims=True)
    spread = jnp.mean(jnp.square(centred), axis=-1, keepdims=True)
    return centred * lax.rsqrt(spread + EPSILON) * gain


def attend(heads, bias):
    rows = heads.shape[0]
    low = lax.broadcasted_iota(jnp.int32, (rows, LANES), 1) < HEAD_DIM
    ones = jnp.ones((rows, LANES), jnp.bfloat16)
    contexts, pending = [], []
    for pair in range(WIDTH // LANES):
        at = pair * LANES
        queries = heads[:, at : at + LANES] * jnp.bfloat16(HEAD_DIM**-0.5)
        keys = heads[:, WIDTH + at : WIDTH + at + LANES]
        values = heads[:, 2 * WIDTH + at : 2 * WIDTH + at + LANES]
        nothing = jnp.zeros_like(queries)
        stacked = jnp.concatenate([jnp.where(low, queries, nothing), jnp.where(low, nothing, queries)], axis=0)
        scores = lax.dot_general(stacked, keys, (((1,), (1,)), ((), ())), preferred_element_type=jnp.float32)
        if bias is not None:
            scores = scores + jnp.concatenate([bias, bias], axis=0)
        weights = jnp.exp(scores - jnp.max(scores, axis=-1, keepdims=True)).astype(jnp.bfloat16)
        pending.append((weights, values))
    for weights, values in pending:
        sums = jnp.dot(weights, jnp.concatenate([values, ones], axis=1), preferred_element_type=jnp.float32)
        context = sums[:, :LANES] / sums[:, LANES:]
        contexts.append(jnp.where(low, context[:rows], context[rows:]))
    return jnp.concatenate(contexts, axis=1).astype(jnp.bfloat16)


def bit_groups():
    inner = lax.axis_size("dev").bit_length() - 1
    bits = inner + lax.axis_size("grp").bit_length() - 1
    return [(inner,), (0, *reversed(range(inner + 1, bits))), tuple(reversed(range(1, inner)))]


def mask_of(index, group):
    return sum(((index >> (len(group) - 1 - at)) & 1) << bit for at, bit in enumerate(group))


def put(parts, scratch, out_refs, groups):
    if groups is None:
        out_refs[0][...] = parts.reshape(out_refs[0].shape)
        return
    scratch[...] = parts
    me = lax.axis_index(AXES)
    order = sum(groups, ())
    size = out_refs[0].shape[0]
    for place in range(size * len(out_refs)):
        out_refs[place // size][place % size, 0] = scratch[mask_of(place, order) ^ me]


def take(ref, groups):
    if groups is None:
        return ref[...]
    me = lax.axis_index(AXES)
    order = sum(groups, ())
    parts = []
    for device in range(ref.shape[0]):
        slot = device ^ me
        place = sum(((slot >> bit) & 1) << (len(order) - 1 - at) for at, bit in enumerate(order))
        parts.append(ref[place, 0])
    return jnp.stack(parts)


def space_first_kernel(
    groups, video_ref, gain_ref, project_ref, output_ref, time_gain_ref, mixed_ref, project, output, *refs
):
    *sent_refs, frame, gains, scratch, sems = refs
    parts = sent_refs[0].shape[0]
    frame_copy = pltpu.make_async_copy(video_ref.at[0], frame, sems.at[0])
    gain_copy = pltpu.make_async_copy(gain_ref, gains.at[pl.ds(0, 1)], sems.at[1])
    weight_copies = [
        pltpu.make_async_copy(project_ref, project, sems.at[2]),
        pltpu.make_async_copy(output_ref, output, sems.at[3]),
        pltpu.make_async_copy(time_gain_ref, gains.at[pl.ds(1, 1)], sems.at[4]),
    ]
    for copy in (gain_copy, frame_copy, weight_copies[0]):
        copy.start()
    gain_copy.wait()
    frame_copy.wait()
    for copy in weight_copies[1:]:
        copy.start()
    floats = frame[...].astype(jnp.float32)
    rows = normed(floats, gains[0:1]).astype(jnp.bfloat16)
    weight_copies[0].wait()
    heads = jnp.dot(rows, project[...], preferred_element_type=jnp.float32).astype(jnp.bfloat16)
    context = attend(heads, None)
    for copy in weight_copies[1:]:
        copy.wait()
    here = (floats + jnp.dot(context, output[...], preferred_element_type=jnp.float32)).astype(jnp.bfloat16)
    mixed_ref[0] = here
    sent = normed(here.astype(jnp.float32), gains[1:2])
    put(sent.reshape(scratch.shape).astype(jnp.bfloat16), scratch, sent_refs, groups)


def space_kernel(groups, extra, video_ref, gain_ref, project_ref, output_ref, time_gain_ref, *refs):
    if extra:
        before_ref, stored_ref, *refs = refs

        @pl.when(pl.program_id(0) == 0)
        def _():
            stored_ref[...] = before_ref[...]

    mixed_ref, *sent_refs = refs
    sent_refs, scratch = (sent_refs, None) if groups is None else (sent_refs[:-1], sent_refs[-1])
    floats = video_ref[0].astype(jnp.float32)
    heads = jnp.dot(
        normed(floats, gain_ref[...]).astype(jnp.bfloat16), project_ref[...], preferred_element_type=jnp.float32
    ).astype(jnp.bfloat16)
    context = attend(heads, None)
    mixed = (floats + jnp.dot(context, output_ref[...], preferred_element_type=jnp.float32)).astype(jnp.bfloat16)
    mixed_ref[0] = mixed
    sent = normed(mixed.astype(jnp.float32), time_gain_ref[...])
    shape = sent_refs[0].shape if groups is None else scratch.shape
    put(sent.reshape(shape).astype(jnp.bfloat16), scratch, sent_refs, groups)


def time_kernel(groups, back, extra, patch_here, rows_ref, project_ref, *refs):
    *context_refs, bias_ref = refs[extra:]
    context_refs, scratch = (context_refs, None) if back is None else (context_refs[:-1], context_refs[-1])
    rows, width = bias_ref.shape[0], rows_ref.shape[-1]

    @pl.when(pl.program_id(0) == 0)
    def _():
        query = lax.broadcasted_iota(jnp.int32, (rows, rows), 0)
        key = lax.broadcasted_iota(jnp.int32, (rows, rows), 1)
        seen = (key <= query) & (lax.rem(query, patch_here) == lax.rem(key, patch_here))
        bias_ref[...] = jnp.where(seen, 0.0, MASKED)

    arrived = take(rows_ref, groups).astype(jnp.float32).reshape(rows, width).astype(jnp.bfloat16)
    heads = jnp.dot(arrived, project_ref[...], preferred_element_type=jnp.float32).astype(jnp.bfloat16)
    context = attend(heads, bias_ref[...]).astype(jnp.float32)
    shape = context_refs[0].shape if back is None else scratch.shape
    put(context.reshape(shape).astype(jnp.bfloat16), scratch, context_refs, back)


def time_wide_kernel(
    patch_here, rows_ref, project_ref, before_ref, context_ref, bias_ref, project, heads, contexts, weight_sems, out_sems
):
    clips, rows, width = heads.shape[0], bias_ref.shape[0], rows_ref.shape[-1]
    tile = heads.shape[2] // weight_sems.shape[0]

    def columns(piece):
        return pl.ds(piece * tile, tile)

    def leaving(clip):
        return pltpu.make_async_copy(contexts.at[clip], context_ref.at[:, clip], out_sems.at[clip])

    weights = [
        pltpu.make_async_copy(project_ref.at[:, columns(piece)], project.at[:, columns(piece)], weight_sems.at[piece])
        for piece in range(weight_sems.shape[0])
    ]
    for copy in weights:
        copy.start()
    query = lax.broadcasted_iota(jnp.int32, (rows, rows), 0)
    key = lax.broadcasted_iota(jnp.int32, (rows, rows), 1)
    seen = (key <= query) & (lax.rem(query, patch_here) == lax.rem(key, patch_here))
    bias_ref[...] = jnp.where(seen, 0.0, MASKED)
    arrived = [rows_ref[:, clip].astype(jnp.float32).reshape(rows, width).astype(jnp.bfloat16) for clip in range(clips)]
    for piece, copy in enumerate(weights):
        copy.wait()
        for at, one in enumerate(arrived):
            got = jnp.dot(one, project[:, columns(piece)], preferred_element_type=jnp.float32).astype(jnp.bfloat16)
            heads[at, :, columns(piece)] = got
    for clip in range(clips):
        context = attend(heads[clip], bias_ref[...])
        contexts[clip] = context.astype(jnp.float32).reshape(contexts.shape[1:]).astype(jnp.bfloat16)
        leaving(clip).start()
    for clip in range(clips):
        leaving(clip).wait()


def final_kernel(order, mixed_ref, context_ref, output_ref, *refs):
    out_ref = refs[-1]
    rows = mixed_ref.shape[1]
    context = take(context_ref, order).astype(jnp.float32).reshape(rows, WIDTH).astype(jnp.bfloat16)
    update = jnp.dot(context, output_ref[...], preferred_element_type=jnp.float32)
    out_ref[0] = (mixed_ref[0].astype(jnp.float32) + update).astype(jnp.bfloat16)


def final_wide_kernel(first, mixed_ref, context_ref, output_ref, before_ref, out_ref, done, sems):
    clips, rows, _ = mixed_ref.shape
    part = rows // SPLIT
    copies = []
    for clip in range(clips):
        context = context_ref[:, clip].astype(jnp.float32).reshape(rows, WIDTH).astype(jnp.bfloat16)
        for at in range(SPLIT):
            here = slice(at * part, (at + 1) * part)
            update = jnp.dot(context[here], output_ref[...], preferred_element_type=jnp.float32)
            done[clip, here] = (mixed_ref[clip, here].astype(jnp.float32) + update).astype(jnp.bfloat16)
            copies.append(
                pltpu.make_async_copy(
                    done.at[clip, pl.ds(at * part, part)],
                    out_ref.at[first + clip, pl.ds(at * part, part)],
                    sems.at[clip, at],
                )
            )
            copies[-1].start()
    for copy in copies:
        copy.wait()


def whole(shape):
    return pl.BlockSpec(shape, lambda c: (0,) * len(shape))


def exchange_spec(count, patch_here, width):
    if patch_here % 8:
        return pl.BlockSpec((1, count * patch_here, width), lambda c: (c, 0, 0))
    return pl.BlockSpec((count, 1, patch_here, width), lambda c: (0, c, 0, 0))


def exchange_shape(count, clips, patch_here, width):
    if patch_here % 8:
        return jax.ShapeDtypeStruct((clips, count * patch_here, width), jnp.bfloat16)
    return jax.ShapeDtypeStruct((count, clips, patch_here, width), jnp.bfloat16)


def exchange(sent, count, patch_here):
    plain = sent.ndim == 3
    if plain:
        clips, _, width = sent.shape
        sent = sent.reshape(clips, count, patch_here, width).transpose(1, 0, 2, 3)
    arrived = lax.all_to_all(sent, AXES, split_axis=0, concat_axis=0, tiled=True)
    if plain:
        arrived = arrived.transpose(1, 0, 2, 3).reshape(clips, count * patch_here, width)
    return arrived


def in_hbm(array):
    return pltpu.with_memory_space_constraint(array, pltpu.HBM)


def in_vmem(array):
    return pltpu.with_memory_space_constraint(array, pltpu.VMEM)


def load_kernel(array_ref, awaited_ref, loaded_ref, sem):
    copy = pltpu.make_async_copy(array_ref, loaded_ref, sem)
    copy.start()
    copy.wait()


def load(array, awaited):
    return pl.pallas_call(
        load_kernel,
        in_specs=[ANYWHERE, ANYWHERE],
        out_specs=pl.BlockSpec(memory_space=pltpu.VMEM),
        out_shape=pltpu.VMEM(array.shape, array.dtype),
        scratch_shapes=[pltpu.SemaphoreType.DMA],
        cost_estimate=cost(0, 4 * array.size, 0),
        compiler_params=pltpu.CompilerParams(vmem_limit_bytes=2 * 1024 * 1024),
        name="load",
    )(in_hbm(array), awaited)


def after(rows, awaited):
    return pl.pallas_call(
        lambda *refs: None,
        in_specs=[ANYWHERE] * (1 + len(awaited)),
        out_specs=ANYWHERE,
        out_shape=jax.ShapeDtypeStruct(rows.shape, rows.dtype),
        input_output_aliases={0: 0},
        compiler_params=pltpu.CompilerParams(vmem_limit_bytes=2 * 1024 * 1024),
        name="after",
    )(in_hbm(rows), *awaited)


def swap(blocks, groups):
    steps = []
    devices = 1 << len(sum(groups, ()))
    rows = blocks[0].shape[1:]
    blocks = [block.reshape(1, *(1 << len(group) for group in groups[1:]), *rows) for block in blocks]
    for at, group in enumerate(groups):
        arrived = [
            lax.ppermute(block, AXES, [(device, device ^ mask_of(index, group)) for device in range(devices)])
            for index, block in enumerate(blocks)
            if index
        ]
        steps.append(arrived)
        whole_buffer = jnp.concatenate([blocks[0], *arrived], axis=at)
        if at + 1 < len(groups):
            blocks = jnp.split(whole_buffer, 1 << len(groups[at + 1]), axis=at + 1)
    return whole_buffer.reshape(devices, *rows), steps


def cost(macs, bytes_accessed, exps):
    return pl.CostEstimate(flops=2 * macs, bytes_accessed=bytes_accessed, transcendentals=exps)


def sent_specs(count, clips, patch_here, width, order):
    if order is None:
        return [exchange_shape(count, clips, patch_here, width)], [exchange_spec(count, patch_here, width)], []
    parts = 1 << len(order[0])
    shape = exchange_shape(count // parts, clips, patch_here, width)
    spec = exchange_spec(count // parts, patch_here, width)
    return [shape] * parts, [spec] * parts, [pltpu.VMEM((count, patch_here, width), jnp.bfloat16)]


def space_call(video, first, clips, space_gain, space_project, space_output, time_gain, count, before, groups):
    rows, width = video.shape[1:]
    vmem = pl.BlockSpec(memory_space=pltpu.VMEM)
    shapes, specs, scratch = sent_specs(count, clips, rows // count, width, groups)
    outputs = pl.pallas_call(
        partial(space_kernel, groups, len(before)),
        grid=(clips,),
        in_specs=[
            pl.BlockSpec((1, rows, width), lambda c: (first + c, 0, 0)),
            whole((1, width)),
            vmem,
            vmem,
            whole((1, width)),
        ]
        + [vmem] * len(before),
        out_specs=[whole((1, rows, width))] * len(before)
        + [pl.BlockSpec((1, rows, width), lambda c: (c, 0, 0)), *specs],
        out_shape=[pltpu.HBM((1, rows, width), jnp.bfloat16)] * len(before)
        + [pltpu.HBM((clips, rows, width), jnp.bfloat16), *(pltpu.HBM(shape.shape, jnp.bfloat16) for shape in shapes)],
        scratch_shapes=scratch,
        cost_estimate=cost(
            clips * rows * (width * 4 * WIDTH + 8 * rows * WIDTH), 2 * (4 * width * WIDTH + 3 * clips * rows * width),
            clips * HEADS * rows * rows,
        ),
        compiler_params=pltpu.CompilerParams(vmem_limit_bytes=SPACE_VMEM_LIMIT),
        name="space",
    )(in_hbm(video), in_hbm(space_gain), in_vmem(space_project), in_vmem(space_output), in_hbm(time_gain), *map(in_vmem, before))
    return outputs[: len(before)], outputs[len(before)], outputs[len(before) + 1 :]


def space_first_call(video, space_gain, space_project, space_output, time_gain, count, groups):
    rows, width = video.shape[1:]
    patch_here = rows // count
    vmem = pl.BlockSpec(memory_space=pltpu.VMEM)
    shapes, _, scratch = sent_specs(count, 1, patch_here, width, groups)
    mixed, project, output, *sent = pl.pallas_call(
        partial(space_first_kernel, groups),
        in_specs=[ANYWHERE] * 5,
        out_specs=[vmem, vmem, vmem, *[vmem] * len(shapes)],
        out_shape=[
            pltpu.VMEM((1, rows, width), jnp.bfloat16),
            pltpu.VMEM(space_project.shape, jnp.bfloat16),
            pltpu.VMEM(space_output.shape, jnp.bfloat16),
            *[pltpu.VMEM(shape.shape, jnp.bfloat16) for shape in shapes],
        ],
        scratch_shapes=[
            pltpu.VMEM((rows, width), jnp.bfloat16),
            pltpu.VMEM((2, width), jnp.float32),
            *scratch,
            pltpu.SemaphoreType.DMA((5,)),
        ],
        cost_estimate=cost(rows * (width * 4 * WIDTH + 8 * rows * WIDTH), 2 * (4 * width * WIDTH + 3 * rows * width), 0),
        compiler_params=pltpu.CompilerParams(vmem_limit_bytes=SPACE_VMEM_LIMIT),
        name="space",
    )(*map(in_hbm, (video, space_gain, space_project, space_output, time_gain)))
    return mixed, project, output, sent


def time_call(arrived, clips, rows, time_project, count, before, groups, back, project=None):
    width = arrived.shape[-1]
    patch_here = rows // count
    shapes, specs, scratch = sent_specs(count, clips, patch_here, WIDTH, back)
    return pl.pallas_call(
        partial(time_kernel, groups, back, len(before), patch_here),
        grid=(clips,),
        in_specs=[exchange_spec(count, patch_here, width), whole((width, 3 * WIDTH)) if project is None else pl.BlockSpec(memory_space=pltpu.VMEM)] + [ANYWHERE] * len(before),
        out_specs=specs,
        out_shape=shapes,
        scratch_shapes=scratch + [pltpu.VMEM((rows, rows), jnp.float32)],
        cost_estimate=cost(
            clips * rows * (width * 3 * WIDTH + 8 * rows * WIDTH), 2 * (3 * width * WIDTH + 2 * clips * rows * width),
            clips * HEADS * rows * rows,
        ),
        compiler_params=pltpu.CompilerParams(vmem_limit_bytes=TIME_VMEM_LIMIT),
        name="time",
    )(arrived, in_hbm(time_project) if project is None else in_vmem(project), *map(in_hbm, before))


def time_wide_call(arrived, clips, rows, time_project, count, before):
    width = arrived.shape[-1]
    patch_here = rows // count
    return pl.pallas_call(
        partial(time_wide_kernel, patch_here),
        in_specs=[pl.BlockSpec(memory_space=pltpu.VMEM), ANYWHERE, ANYWHERE],
        out_specs=ANYWHERE,
        out_shape=pltpu.HBM((count, clips, patch_here, WIDTH), jnp.bfloat16),
        scratch_shapes=[
            pltpu.VMEM((rows, rows), jnp.float32),
            pltpu.VMEM((width, 3 * WIDTH), jnp.bfloat16),
            pltpu.VMEM((clips, rows, 3 * WIDTH), jnp.bfloat16),
            pltpu.VMEM((clips, count, patch_here, WIDTH), jnp.bfloat16),
            pltpu.SemaphoreType.DMA((PIECES,)),
            pltpu.SemaphoreType.DMA((clips,)),
        ],
        cost_estimate=cost(
            clips * rows * (width * 3 * WIDTH + 8 * rows * WIDTH), 2 * (3 * width * WIDTH + 2 * clips * rows * width),
            clips * HEADS * rows * rows,
        ),
        compiler_params=pltpu.CompilerParams(vmem_limit_bytes=TIME_VMEM_LIMIT),
        name="time",
    )(arrived, in_hbm(time_project), in_hbm(before))


def final_call(mixed, context, time_output, count, first, total, before, order):
    clips, rows, width = mixed.shape
    return pl.pallas_call(
        partial(final_kernel, order),
        grid=(clips,),
        in_specs=[
            pl.BlockSpec((1, rows, width), lambda c: (c, 0, 0)),
            exchange_spec(count, rows // count, WIDTH),
            whole((WIDTH, width)),
        ]
        + [ANYWHERE] * len(before),
        out_specs=pl.BlockSpec((1, rows, width), lambda c: (first + c, 0, 0)),
        out_shape=jax.ShapeDtypeStruct((total, rows, width), jnp.bfloat16),
        input_output_aliases={3: 0} if before else {},
        cost_estimate=cost(clips * rows * width * WIDTH, 2 * (width * WIDTH + 3 * clips * rows * width), 0),
        compiler_params=pltpu.CompilerParams(vmem_limit_bytes=FINAL_VMEM_LIMIT),
        name="final",
    )(mixed, context, time_output, *before)


def final_wide_call(mixed, context, time_output, first, total, before):
    clips, rows, width = mixed.shape
    vmem = pl.BlockSpec(memory_space=pltpu.VMEM)
    return pl.pallas_call(
        partial(final_wide_kernel, first),
        in_specs=[vmem, vmem, vmem, ANYWHERE],
        out_specs=ANYWHERE,
        out_shape=jax.ShapeDtypeStruct((total, rows, width), jnp.bfloat16),
        scratch_shapes=[pltpu.VMEM((clips, rows, width), jnp.bfloat16), pltpu.SemaphoreType.DMA((clips, SPLIT))],
        input_output_aliases={3: 0},
        cost_estimate=cost(clips * rows * width * WIDTH, 2 * (width * WIDTH + 3 * clips * rows * width), 0),
        compiler_params=pltpu.CompilerParams(vmem_limit_bytes=FINAL_VMEM_LIMIT),
        name="final",
    )(mixed, context, time_output, before)


def per_device(video_in, space_gain, space_project, space_output, time_gain, time_project, time_output):
    clip_count, frame_local, patch_count, width = video_in.shape
    count = lax.axis_size("grp") * lax.axis_size("dev")
    patch_here = patch_count // count
    video = video_in.reshape(clip_count, patch_count, width)
    weights = space_gain.reshape(1, width), space_project, space_output, time_gain.reshape(1, width)
    swappable = patch_here % 8 == 0 and count & (count - 1) == 0
    if not swappable:
        return plainly(video, weights, time_project, time_output, count).reshape(video_in.shape)
    others = clip_count - 1
    core, near, far = bit_groups()
    there, back = [far, core, near], [near, far, core]
    kept, project, output, sent = space_first_call(video, *weights, count, there)
    weights = weights[0], project, output, weights[3]
    (kept,), kept_others, sent_others = space_call(video, 1, others, *weights, count, [kept], None)
    arrived, steps = swap(sent, there)
    arrived_others = exchange(after(sent_others[0], steps[0]), count, patch_here)
    loaded = load(time_project, steps[1][0])
    context = time_call(arrived, 1, patch_count, time_project, count, [], there, back, loaded)
    returned, steps = swap(context, back)
    context = time_wide_call(arrived_others, others, patch_count, time_project, count, context[0])
    returned_others = exchange(after(context, steps[1]), count, patch_here)
    out = final_call(kept, returned, time_output, count, 0, clip_count, [], back)
    out = final_wide_call(kept_others, returned_others, time_output, 1, clip_count, out)
    return out.reshape(clip_count, frame_local, patch_count, width)


def plainly(video, weights, time_project, time_output, count):
    clips, rows, _ = video.shape
    _, kept, sent = space_call(video, 0, clips, *weights, count, [], None)
    arrived = exchange(sent[0], count, rows // count)
    context = time_call(arrived, clips, rows, time_project, count, [], None, None)
    returned = exchange(context[0], count, rows // count)
    return final_call(kept, returned, time_output, count, 0, clips, [], None)


def solution(mesh):
    in_specs = (P(None, AXES, None, None), P(), P(), P(), P(), P(), P())
    return jax.shard_map(
        per_device, mesh=mesh, in_specs=in_specs, out_specs=P(None, AXES, None, None), check_vma=False
    )
```

```python
from functools import partial

import jax
import jax.numpy as jnp
from jax import lax
from jax.experimental import pallas as pl
from jax.experimental.pallas import tpu as pltpu
from jax.sharding import PartitionSpec as P

HEADS = 8
HEAD_DIM = 64
WIDTH = HEADS * HEAD_DIM
LANES = 128
EPSILON = 1e-06
MASKED = -1e30
SPACE_VMEM_LIMIT = 40 * 1024 * 1024
SPLIT = 2
PIECES = 3
ANYWHERE = pl.BlockSpec(memory_space=pl.ANY)
AXES = ("grp", "dev")
VMEM_LIMIT = 60 * 1024 * 1024
TIME_VMEM_LIMIT = 40 * 1024 * 1024
FINAL_VMEM_LIMIT = 40 * 1024 * 1024


def normed(floats, gain):
    centred = floats - jnp.mean(floats, axis=-1, keepdims=True)
    spread = jnp.mean(jnp.square(centred), axis=-1, keepdims=True)
    return centred * lax.rsqrt(spread + EPSILON) * gain


def attend(heads, bias):
    rows = heads.shape[0]
    low = lax.broadcasted_iota(jnp.int32, (rows, LANES), 1) < HEAD_DIM
    nothing = jnp.zeros((rows, LANES), jnp.bfloat16)
    ones = jnp.ones((rows, LANES), jnp.bfloat16)

    def apart(tile):
        return jnp.concatenate([jnp.where(low, tile, nothing), jnp.where(low, nothing, tile)], axis=0)

    ones = apart(ones)
    contexts, pending = [], []
    for pair in range(WIDTH // LANES):
        at = pair * LANES
        queries = heads[:, at : at + LANES] * jnp.bfloat16(HEAD_DIM**-0.5)
        keys = apart(heads[:, WIDTH + at : WIDTH + at + LANES])
        values = apart(heads[:, 2 * WIDTH + at : 2 * WIDTH + at + LANES])
        scores = lax.dot_general(queries, keys, (((1,), (1,)), ((), ())), preferred_element_type=jnp.float32)
        weights = []
        for one in (scores[:, :rows], scores[:, rows:]):
            if bias is not None:
                one = one + bias
            weights.append(jnp.exp(one - jnp.max(one, axis=-1, keepdims=True)).astype(jnp.bfloat16))
        pending.append((weights, values))
    for weights, values in pending:
        sums = jnp.dot(
            jnp.concatenate(weights, axis=1), jnp.concatenate([values, ones], axis=1), preferred_element_type=jnp.float32
        )
        contexts.append(sums[:, :LANES] / sums[:, LANES:])
    return jnp.concatenate(contexts, axis=1).astype(jnp.bfloat16)


def bit_groups():
    inner = lax.axis_size("dev").bit_length() - 1
    bits = inner + lax.axis_size("grp").bit_length() - 1
    return [(inner,), (0, *reversed(range(inner + 1, bits))), tuple(reversed(range(1, inner)))]


def mask_of(index, group):
    return sum(((index >> (len(group) - 1 - at)) & 1) << bit for at, bit in enumerate(group))


def put(parts, scratch, out_refs, groups):
    if groups is None:
        out_refs[0][...] = parts.reshape(out_refs[0].shape)
        return
    scratch[...] = parts
    me = lax.axis_index(AXES)
    order = sum(groups, ())
    size = out_refs[0].shape[0]
    for place in range(size * len(out_refs)):
        out_refs[place // size][place % size, 0] = scratch[mask_of(place, order) ^ me]


def take(ref, groups):
    if groups is None:
        return ref[...]
    me = lax.axis_index(AXES)
    order = sum(groups, ())
    parts = []
    for device in range(ref.shape[0]):
        slot = device ^ me
        place = sum(((slot >> bit) & 1) << (len(order) - 1 - at) for at, bit in enumerate(order))
        parts.append(ref[place, 0])
    return jnp.stack(parts)


def space_first_kernel(
    groups, video_ref, gain_ref, project_ref, output_ref, time_gain_ref, mixed_ref, project, output, *refs
):
    *sent_refs, frame, gains, scratch, sems = refs
    parts = sent_refs[0].shape[0]
    frame_copy = pltpu.make_async_copy(video_ref.at[0], frame, sems.at[0])
    gain_copy = pltpu.make_async_copy(gain_ref, gains.at[pl.ds(0, 1)], sems.at[1])
    weight_copies = [
        pltpu.make_async_copy(project_ref, project, sems.at[2]),
        pltpu.make_async_copy(output_ref, output, sems.at[3]),
        pltpu.make_async_copy(time_gain_ref, gains.at[pl.ds(1, 1)], sems.at[4]),
    ]
    for copy in (gain_copy, frame_copy, weight_copies[0]):
        copy.start()
    gain_copy.wait()
    frame_copy.wait()
    for copy in weight_copies[1:]:
        copy.start()
    floats = frame[...].astype(jnp.float32)
    rows = normed(floats, gains[0:1]).astype(jnp.bfloat16)
    weight_copies[0].wait()
    heads = jnp.dot(rows, project[...], preferred_element_type=jnp.float32).astype(jnp.bfloat16)
    context = attend(heads, None)
    for copy in weight_copies[1:]:
        copy.wait()
    here = (floats + jnp.dot(context, output[...], preferred_element_type=jnp.float32)).astype(jnp.bfloat16)
    mixed_ref[0] = here
    sent = normed(here.astype(jnp.float32), gains[1:2])
    put(sent.reshape(scratch.shape).astype(jnp.bfloat16), scratch, sent_refs, groups)


def space_kernel(groups, extra, video_ref, gain_ref, project_ref, output_ref, time_gain_ref, *refs):
    if extra:
        before_ref, stored_ref, *refs = refs

        @pl.when(pl.program_id(0) == 0)
        def _():
            stored_ref[...] = before_ref[...]

    mixed_ref, *sent_refs = refs
    sent_refs, scratch = (sent_refs, None) if groups is None else (sent_refs[:-1], sent_refs[-1])
    floats = video_ref[0].astype(jnp.float32)
    heads = jnp.dot(
        normed(floats, gain_ref[...]).astype(jnp.bfloat16), project_ref[...], preferred_element_type=jnp.float32
    ).astype(jnp.bfloat16)
    context = attend(heads, None)
    mixed = (floats + jnp.dot(context, output_ref[...], preferred_element_type=jnp.float32)).astype(jnp.bfloat16)
    mixed_ref[0] = mixed
    sent = normed(mixed.astype(jnp.float32), time_gain_ref[...])
    shape = sent_refs[0].shape if groups is None else scratch.shape
    put(sent.reshape(shape).astype(jnp.bfloat16), scratch, sent_refs, groups)


def time_kernel(groups, back, extra, patch_here, rows_ref, project_ref, *refs):
    *context_refs, bias_ref = refs[extra:]
    context_refs, scratch = (context_refs, None) if back is None else (context_refs[:-1], context_refs[-1])
    rows, width = bias_ref.shape[0], rows_ref.shape[-1]

    @pl.when(pl.program_id(0) == 0)
    def _():
        query = lax.broadcasted_iota(jnp.int32, (rows, rows), 0)
        key = lax.broadcasted_iota(jnp.int32, (rows, rows), 1)
        seen = (key <= query) & (lax.rem(query, patch_here) == lax.rem(key, patch_here))
        bias_ref[...] = jnp.where(seen, 0.0, MASKED)

    arrived = take(rows_ref, groups).astype(jnp.float32).reshape(rows, width).astype(jnp.bfloat16)
    heads = jnp.dot(arrived, project_ref[...], preferred_element_type=jnp.float32).astype(jnp.bfloat16)
    context = attend(heads, bias_ref[...]).astype(jnp.float32)
    shape = context_refs[0].shape if back is None else scratch.shape
    put(context.reshape(shape).astype(jnp.bfloat16), scratch, context_refs, back)


def time_wide_kernel(
    patch_here, rows_ref, project_ref, before_ref, context_ref, bias_ref, project, heads, contexts, weight_sems, out_sems
):
    clips, rows, width = heads.shape[0], bias_ref.shape[0], rows_ref.shape[-1]
    tile = heads.shape[2] // weight_sems.shape[0]

    def columns(piece):
        return pl.ds(piece * tile, tile)

    def leaving(clip):
        return pltpu.make_async_copy(contexts.at[clip], context_ref.at[:, clip], out_sems.at[clip])

    weights = [
        pltpu.make_async_copy(project_ref.at[:, columns(piece)], project.at[:, columns(piece)], weight_sems.at[piece])
        for piece in range(weight_sems.shape[0])
    ]
    for copy in weights:
        copy.start()
    query = lax.broadcasted_iota(jnp.int32, (rows, rows), 0)
    key = lax.broadcasted_iota(jnp.int32, (rows, rows), 1)
    seen = (key <= query) & (lax.rem(query, patch_here) == lax.rem(key, patch_here))
    bias_ref[...] = jnp.where(seen, 0.0, MASKED)
    arrived = [rows_ref[:, clip].astype(jnp.float32).reshape(rows, width).astype(jnp.bfloat16) for clip in range(clips)]
    for piece, copy in enumerate(weights):
        copy.wait()
        for at, one in enumerate(arrived):
            got = jnp.dot(one, project[:, columns(piece)], preferred_element_type=jnp.float32).astype(jnp.bfloat16)
            heads[at, :, columns(piece)] = got
    for clip in range(clips):
        context = attend(heads[clip], bias_ref[...])
        contexts[clip] = context.astype(jnp.float32).reshape(contexts.shape[1:]).astype(jnp.bfloat16)
        leaving(clip).start()
    for clip in range(clips):
        leaving(clip).wait()


def final_kernel(order, mixed_ref, context_ref, output_ref, *refs):
    out_ref = refs[-1]
    rows = mixed_ref.shape[1]
    context = take(context_ref, order).astype(jnp.float32).reshape(rows, WIDTH).astype(jnp.bfloat16)
    update = jnp.dot(context, output_ref[...], preferred_element_type=jnp.float32)
    out_ref[0] = (mixed_ref[0].astype(jnp.float32) + update).astype(jnp.bfloat16)


def final_wide_kernel(first, mixed_ref, context_ref, output_ref, before_ref, out_ref, done, sems):
    clips, rows, _ = mixed_ref.shape
    part = rows // SPLIT
    copies = []
    for clip in range(clips):
        context = context_ref[:, clip].astype(jnp.float32).reshape(rows, WIDTH).astype(jnp.bfloat16)
        for at in range(SPLIT):
            here = slice(at * part, (at + 1) * part)
            update = jnp.dot(context[here], output_ref[...], preferred_element_type=jnp.float32)
            done[clip, here] = (mixed_ref[clip, here].astype(jnp.float32) + update).astype(jnp.bfloat16)
            copies.append(
                pltpu.make_async_copy(
                    done.at[clip, pl.ds(at * part, part)],
                    out_ref.at[first + clip, pl.ds(at * part, part)],
                    sems.at[clip, at],
                )
            )
            copies[-1].start()
    for copy in copies:
        copy.wait()


def whole(shape):
    return pl.BlockSpec(shape, lambda c: (0,) * len(shape))


def exchange_spec(count, patch_here, width):
    if patch_here % 8:
        return pl.BlockSpec((1, count * patch_here, width), lambda c: (c, 0, 0))
    return pl.BlockSpec((count, 1, patch_here, width), lambda c: (0, c, 0, 0))


def exchange_shape(count, clips, patch_here, width):
    if patch_here % 8:
        return jax.ShapeDtypeStruct((clips, count * patch_here, width), jnp.bfloat16)
    return jax.ShapeDtypeStruct((count, clips, patch_here, width), jnp.bfloat16)


def exchange(sent, count, patch_here):
    plain = sent.ndim == 3
    if plain:
        clips, _, width = sent.shape
        sent = sent.reshape(clips, count, patch_here, width).transpose(1, 0, 2, 3)
    arrived = lax.all_to_all(sent, AXES, split_axis=0, concat_axis=0, tiled=True)
    if plain:
        arrived = arrived.transpose(1, 0, 2, 3).reshape(clips, count * patch_here, width)
    return arrived


def in_hbm(array):
    return pltpu.with_memory_space_constraint(array, pltpu.HBM)


def in_vmem(array):
    return pltpu.with_memory_space_constraint(array, pltpu.VMEM)


def load_kernel(array_ref, awaited_ref, loaded_ref, sem):
    copy = pltpu.make_async_copy(array_ref, loaded_ref, sem)
    copy.start()
    copy.wait()


def load(array, awaited):
    return pl.pallas_call(
        load_kernel,
        in_specs=[ANYWHERE, ANYWHERE],
        out_specs=pl.BlockSpec(memory_space=pltpu.VMEM),
        out_shape=pltpu.VMEM(array.shape, array.dtype),
        scratch_shapes=[pltpu.SemaphoreType.DMA],
        cost_estimate=cost(0, 4 * array.size, 0),
        compiler_params=pltpu.CompilerParams(vmem_limit_bytes=2 * 1024 * 1024),
        name="load",
    )(in_hbm(array), awaited)


def after(rows, awaited):
    return pl.pallas_call(
        lambda *refs: None,
        in_specs=[ANYWHERE] * (1 + len(awaited)),
        out_specs=ANYWHERE,
        out_shape=jax.ShapeDtypeStruct(rows.shape, rows.dtype),
        input_output_aliases={0: 0},
        compiler_params=pltpu.CompilerParams(vmem_limit_bytes=2 * 1024 * 1024),
        name="after",
    )(in_hbm(rows), *awaited)


def swap(blocks, groups):
    steps = []
    devices = 1 << len(sum(groups, ()))
    rows = blocks[0].shape[1:]
    blocks = [block.reshape(1, *(1 << len(group) for group in groups[1:]), *rows) for block in blocks]
    for at, group in enumerate(groups):
        arrived = [
            lax.ppermute(block, AXES, [(device, device ^ mask_of(index, group)) for device in range(devices)])
            for index, block in enumerate(blocks)
            if index
        ]
        steps.append(arrived)
        whole_buffer = jnp.concatenate([blocks[0], *arrived], axis=at)
        if at + 1 < len(groups):
            blocks = jnp.split(whole_buffer, 1 << len(groups[at + 1]), axis=at + 1)
    return whole_buffer.reshape(devices, *rows), steps


def cost(macs, bytes_accessed, exps):
    return pl.CostEstimate(flops=2 * macs, bytes_accessed=bytes_accessed, transcendentals=exps)


def sent_specs(count, clips, patch_here, width, order):
    if order is None:
        return [exchange_shape(count, clips, patch_here, width)], [exchange_spec(count, patch_here, width)], []
    parts = 1 << len(order[0])
    shape = exchange_shape(count // parts, clips, patch_here, width)
    spec = exchange_spec(count // parts, patch_here, width)
    return [shape] * parts, [spec] * parts, [pltpu.VMEM((count, patch_here, width), jnp.bfloat16)]


def space_call(video, first, clips, space_gain, space_project, space_output, time_gain, count, before, groups):
    rows, width = video.shape[1:]
    vmem = pl.BlockSpec(memory_space=pltpu.VMEM)
    shapes, specs, scratch = sent_specs(count, clips, rows // count, width, groups)
    outputs = pl.pallas_call(
        partial(space_kernel, groups, len(before)),
        grid=(clips,),
        in_specs=[
            pl.BlockSpec((1, rows, width), lambda c: (first + c, 0, 0)),
            whole((1, width)),
            vmem,
            vmem,
            whole((1, width)),
        ]
        + [vmem] * len(before),
        out_specs=[whole((1, rows, width))] * len(before)
        + [pl.BlockSpec((1, rows, width), lambda c: (c, 0, 0)), *specs],
        out_shape=[pltpu.HBM((1, rows, width), jnp.bfloat16)] * len(before)
        + [pltpu.HBM((clips, rows, width), jnp.bfloat16), *(pltpu.HBM(shape.shape, jnp.bfloat16) for shape in shapes)],
        scratch_shapes=scratch,
        cost_estimate=cost(
            clips * rows * (width * 4 * WIDTH + 8 * rows * WIDTH), 2 * (4 * width * WIDTH + 3 * clips * rows * width),
            clips * HEADS * rows * rows,
        ),
        compiler_params=pltpu.CompilerParams(vmem_limit_bytes=SPACE_VMEM_LIMIT),
        name="space",
    )(in_hbm(video), in_hbm(space_gain), in_vmem(space_project), in_vmem(space_output), in_hbm(time_gain), *map(in_vmem, before))
    return outputs[: len(before)], outputs[len(before)], outputs[len(before) + 1 :]


def space_first_call(video, space_gain, space_project, space_output, time_gain, count, groups):
    rows, width = video.shape[1:]
    patch_here = rows // count
    vmem = pl.BlockSpec(memory_space=pltpu.VMEM)
    shapes, _, scratch = sent_specs(count, 1, patch_here, width, groups)
    mixed, project, output, *sent = pl.pallas_call(
        partial(space_first_kernel, groups),
        in_specs=[ANYWHERE] * 5,
        out_specs=[vmem, vmem, vmem, *[vmem] * len(shapes)],
        out_shape=[
            pltpu.VMEM((1, rows, width), jnp.bfloat16),
            pltpu.VMEM(space_project.shape, jnp.bfloat16),
            pltpu.VMEM(space_output.shape, jnp.bfloat16),
            *[pltpu.VMEM(shape.shape, jnp.bfloat16) for shape in shapes],
        ],
        scratch_shapes=[
            pltpu.VMEM((rows, width), jnp.bfloat16),
            pltpu.VMEM((2, width), jnp.float32),
            *scratch,
            pltpu.SemaphoreType.DMA((5,)),
        ],
        cost_estimate=cost(rows * (width * 4 * WIDTH + 8 * rows * WIDTH), 2 * (4 * width * WIDTH + 3 * rows * width), 0),
        compiler_params=pltpu.CompilerParams(vmem_limit_bytes=SPACE_VMEM_LIMIT),
        name="space",
    )(*map(in_hbm, (video, space_gain, space_project, space_output, time_gain)))
    return mixed, project, output, sent


def time_call(arrived, clips, rows, time_project, count, before, groups, back, project=None):
    width = arrived.shape[-1]
    patch_here = rows // count
    shapes, specs, scratch = sent_specs(count, clips, patch_here, WIDTH, back)
    return pl.pallas_call(
        partial(time_kernel, groups, back, len(before), patch_here),
        grid=(clips,),
        in_specs=[exchange_spec(count, patch_here, width), whole((width, 3 * WIDTH)) if project is None else pl.BlockSpec(memory_space=pltpu.VMEM)] + [ANYWHERE] * len(before),
        out_specs=specs,
        out_shape=shapes,
        scratch_shapes=scratch + [pltpu.VMEM((rows, rows), jnp.float32)],
        cost_estimate=cost(
            clips * rows * (width * 3 * WIDTH + 8 * rows * WIDTH), 2 * (3 * width * WIDTH + 2 * clips * rows * width),
            clips * HEADS * rows * rows,
        ),
        compiler_params=pltpu.CompilerParams(vmem_limit_bytes=TIME_VMEM_LIMIT),
        name="time",
    )(arrived, in_hbm(time_project) if project is None else in_vmem(project), *map(in_hbm, before))


def time_wide_call(arrived, clips, rows, time_project, count, before):
    width = arrived.shape[-1]
    patch_here = rows // count
    return pl.pallas_call(
        partial(time_wide_kernel, patch_here),
        in_specs=[pl.BlockSpec(memory_space=pltpu.VMEM), ANYWHERE, ANYWHERE],
        out_specs=ANYWHERE,
        out_shape=pltpu.HBM((count, clips, patch_here, WIDTH), jnp.bfloat16),
        scratch_shapes=[
            pltpu.VMEM((rows, rows), jnp.float32),
            pltpu.VMEM((width, 3 * WIDTH), jnp.bfloat16),
            pltpu.VMEM((clips, rows, 3 * WIDTH), jnp.bfloat16),
            pltpu.VMEM((clips, count, patch_here, WIDTH), jnp.bfloat16),
            pltpu.SemaphoreType.DMA((PIECES,)),
            pltpu.SemaphoreType.DMA((clips,)),
        ],
        cost_estimate=cost(
            clips * rows * (width * 3 * WIDTH + 8 * rows * WIDTH), 2 * (3 * width * WIDTH + 2 * clips * rows * width),
            clips * HEADS * rows * rows,
        ),
        compiler_params=pltpu.CompilerParams(vmem_limit_bytes=TIME_VMEM_LIMIT),
        name="time",
    )(arrived, in_hbm(time_project), in_hbm(before))


def final_call(mixed, context, time_output, count, first, total, before, order):
    clips, rows, width = mixed.shape
    return pl.pallas_call(
        partial(final_kernel, order),
        grid=(clips,),
        in_specs=[
            pl.BlockSpec((1, rows, width), lambda c: (c, 0, 0)),
            exchange_spec(count, rows // count, WIDTH),
            whole((WIDTH, width)),
        ]
        + [ANYWHERE] * len(before),
        out_specs=pl.BlockSpec((1, rows, width), lambda c: (first + c, 0, 0)),
        out_shape=jax.ShapeDtypeStruct((total, rows, width), jnp.bfloat16),
        input_output_aliases={3: 0} if before else {},
        cost_estimate=cost(clips * rows * width * WIDTH, 2 * (width * WIDTH + 3 * clips * rows * width), 0),
        compiler_params=pltpu.CompilerParams(vmem_limit_bytes=FINAL_VMEM_LIMIT),
        name="final",
    )(mixed, context, time_output, *before)


def final_wide_call(mixed, context, time_output, first, total, before):
    clips, rows, width = mixed.shape
    vmem = pl.BlockSpec(memory_space=pltpu.VMEM)
    return pl.pallas_call(
        partial(final_wide_kernel, first),
        in_specs=[vmem, vmem, vmem, ANYWHERE],
        out_specs=ANYWHERE,
        out_shape=jax.ShapeDtypeStruct((total, rows, width), jnp.bfloat16),
        scratch_shapes=[pltpu.VMEM((clips, rows, width), jnp.bfloat16), pltpu.SemaphoreType.DMA((clips, SPLIT))],
        input_output_aliases={3: 0},
        cost_estimate=cost(clips * rows * width * WIDTH, 2 * (width * WIDTH + 3 * clips * rows * width), 0),
        compiler_params=pltpu.CompilerParams(vmem_limit_bytes=FINAL_VMEM_LIMIT),
        name="final",
    )(mixed, context, time_output, before)


def per_device(video_in, space_gain, space_project, space_output, time_gain, time_project, time_output):
    clip_count, frame_local, patch_count, width = video_in.shape
    count = lax.axis_size("grp") * lax.axis_size("dev")
    patch_here = patch_count // count
    video = video_in.reshape(clip_count, patch_count, width)
    weights = space_gain.reshape(1, width), space_project, space_output, time_gain.reshape(1, width)
    swappable = patch_here % 8 == 0 and count & (count - 1) == 0
    if not swappable:
        return plainly(video, weights, time_project, time_output, count).reshape(video_in.shape)
    others = clip_count - 1
    core, near, far = bit_groups()
    there, back = [far, core, near], [near, far, core]
    kept, project, output, sent = space_first_call(video, *weights, count, there)
    weights = weights[0], project, output, weights[3]
    (kept,), kept_others, sent_others = space_call(video, 1, others, *weights, count, [kept], None)
    arrived, steps = swap(sent, there)
    arrived_others = exchange(after(sent_others[0], steps[0]), count, patch_here)
    loaded = load(time_project, steps[1][0])
    context = time_call(arrived, 1, patch_count, time_project, count, [], there, back, loaded)
    returned, steps = swap(context, back)
    context = time_wide_call(arrived_others, others, patch_count, time_project, count, context[0])
    returned_others = exchange(after(context, steps[1]), count, patch_here)
    out = final_call(kept, returned, time_output, count, 0, clip_count, [], back)
    out = final_wide_call(kept_others, returned_others, time_output, 1, clip_count, out)
    return out.reshape(clip_count, frame_local, patch_count, width)


def plainly(video, weights, time_project, time_output, count):
    clips, rows, _ = video.shape
    _, kept, sent = space_call(video, 0, clips, *weights, count, [], None)
    arrived = exchange(sent[0], count, rows // count)
    context = time_call(arrived, clips, rows, time_project, count, [], None, None)
    returned = exchange(context[0], count, rows // count)
    return final_call(kept, returned, time_output, count, 0, clips, [], None)


def solution(mesh):
    in_specs = (P(None, AXES, None, None), P(), P(), P(), P(), P(), P())
    return jax.shard_map(
        per_device, mesh=mesh, in_specs=in_specs, out_specs=P(None, AXES, None, None), check_vma=False
    )
```
